256 devices in a mesh: tm: 16 (over y, x_hi, core), space: 16 (over z, x_lo).
Axes of the slice: x: 4 (x_hi: 2, x_lo: 2; x = x_hi * 2 + x_lo), y: 4, z: 8, core: 2. Of those that a mesh axis runs over, the one named last changes fastest.
Arguments:
- frames: bfloat16 [128, 16, 16, 2048], P('tm', 'space'), may hold values from -24 to 24
- actions: int32 [128], P('tm'), may hold values from 0 to 7
- action_table: bfloat16 [8, 2048], replicated, may hold values from -5 to 5
- norm_gain: float32 [2048], replicated, may hold values from 0.1 to 1.9
- w_q: bfloat16 [2048, 2048], P(None, 'space'), may hold values from -0.125 to 0.125
- w_kv: bfloat16 [2048, 2, 128], P(None, None, 'space'), may hold values from -0.125 to 0.125
- qk_gain: float32 [2, 128], replicated, may hold values from 0.5 to 10
- w_o: bfloat16 [2048, 2048], P('space'), may hold values from -0.5 to 0.5
- w_up: bfloat16 [2048, 8192], P(None, 'space'), may hold values from -0.125 to 0.125
- w_down: bfloat16 [8192, 2048], P('space'), may hold values from -0.0625 to 0.0625
- w_lat: bfloat16 [2048, 512], replicated, may hold values from -0.125 to 0.125
- w_conv: bfloat16 [3, 3, 512, 512], replicated, may hold values from -0.1875 to 0.1875
- conv_bias: float32 [512], replicated, may hold values from -3 to 3
Outputs:
- decoded: bfloat16 [128, 32, 32, 512], P('tm', 'space')
The draws below stay inside these ranges and needn't reach their ends.
All inputs are finite; a program needn't handle non-finite values.
Results may differ from the reference program's by a relative error of at most 0.025.
The reference program's roundings to bfloat16 on the way count: a program that leaves them out, or rounds other values in their place, can miss the bound.
Values may be sent and summed in bfloat16 or wider, within the bound.
A program may use at most 192 MiB of HBM per device.

```python
import math
import jax
import jax.numpy as jnp
from jax import lax

D = 2048
HEADS = 16
FF = 8192
C = 512
ACTS = 8
GH = 16
GW = 16
F = 128
HD = 128
N_SPACE = 16


def draw_frames(key, part):
    key = jax.random.fold_in(key, 11)
    base_key, row_key, column_key = jax.random.split(key, 3)
    base = jax.random.truncated_normal(base_key, -4.0, 4.0, (F, GH, GW, D), jnp.float32)
    row_scale = jnp.exp(jax.random.uniform(row_key, (F, GH, GW, 1), jnp.float32, math.log(0.3), math.log(3.0)))
    column_scale = jnp.exp(jax.random.uniform(column_key, (D,), jnp.float32, math.log(0.4), math.log(4.0)))
    return jnp.clip(base * row_scale * column_scale, -24.0, 24.0).astype(jnp.bfloat16)


def draw_qk_gain(key, part):
    key = jax.random.fold_in(key, 7)
    lowest = 0.5
    highest = 2.0
    gains = jnp.exp(jax.random.uniform(key, (2, HD), jnp.float32, math.log(lowest), math.log(highest)))
    return jnp.clip(gains, 0.5, 10.0)


def place_ends(result, key, low, high):
    longest = result.shape.index(max(result.shape))
    spots = []
    for shift in (0, 1):
        where = [jax.random.randint(jax.random.fold_in(key, axis), (), 0, length) for axis, length in enumerate(result.shape)]
        where[longest] = (where[longest] + shift) % result.shape[longest]
        spots.append(tuple(where))
    return result.at[spots[0]].set(low).at[spots[1]].set(high)


def levels(stream_key, extent, cuts, least, high):
    loudness = 1.0
    for position, shards_of in cuts:
        heights = jax.random.uniform(jax.random.fold_in(jax.random.fold_in(stream_key, 6), position), (shards_of,), jnp.float32, least / len(cuts), high / len(cuts))
        loudness = loudness * jnp.repeat(jnp.exp(heights), extent[position] // shards_of).reshape((-1,) + (1,) * (len(extent) - 1 - position))
    return loudness


def bell_draw(key, extent, spread, most, pieces=(), kind=jnp.bfloat16):
    array = spread * jax.random.normal(key, extent, jnp.float32)
    if pieces:
        array = array * levels(key, extent, pieces, -0.22, 0.18)
    return jnp.clip(array, -most, most).astype(kind)


def setup_inputs(seed: int = 0) -> dict:
    arg_keys = jax.random.split(jax.random.key(seed), 14)
    frames = draw_frames(jax.random.fold_in(arg_keys[13], 71), 0)
    actions = place_ends(jax.random.randint(arg_keys[1], (F,), 0, ACTS), jax.random.fold_in(arg_keys[1], 1), 0, ACTS - 1).astype(jnp.int32)
    action_table = bell_draw(arg_keys[2], (ACTS, D), 1.0, 5.0)
    norm_gain = jnp.clip(1.0 + 0.18 * jax.random.normal(arg_keys[3], (D,), jnp.float32), 0.1, 1.9)
    w_q = bell_draw(arg_keys[4], (D, D), D ** -0.5, 0.125, ((1, 16),))
    w_kv = bell_draw(arg_keys[5], (D, 2, HD), D ** -0.5, 0.125, ((2, 16),))
    qk_gain = draw_qk_gain(jax.random.fold_in(arg_keys[13], 71), 0)
    w_o = bell_draw(arg_keys[7], (D, D), HD ** -0.5, 0.5, ((0, 16),))
    w_up = bell_draw(arg_keys[8], (D, FF), D ** -0.5, 0.125, ((1, 16),))
    w_down = bell_draw(arg_keys[9], (FF, D), FF ** -0.5, 0.0625, ((0, 16),))
    w_lat = bell_draw(arg_keys[10], (D, C), D ** -0.5, 0.125)
    w_conv = bell_draw(arg_keys[11], (3, 3, C, C), (2 * C) ** -0.5, 0.1875)
    conv_bias = bell_draw(arg_keys[12], (C,), 0.5, 3.0, (), jnp.float32)
    return {"frames": frames, "actions": actions, "action_table": action_table, "norm_gain": norm_gain, "w_q": w_q, "w_kv": w_kv, "qk_gain": qk_gain, "w_o": w_o, "w_up": w_up, "w_down": w_down, "w_lat": w_lat, "w_conv": w_conv, "conv_bias": conv_bias}


epsilon = 1e-06

def root_scale(values, gain):
    return values * lax.rsqrt(lax.optimization_barrier(jnp.mean(values * values, axis=-1, keepdims=True)) + epsilon) * gain

def tap_product(cells, kernel):
    flat_cells = cells.reshape(-1, cells.shape[-1])
    return jnp.dot(flat_cells, kernel, preferred_element_type=jnp.float32).reshape(cells.shape[:-1] + (kernel.shape[1],))

def reference(frames, actions, action_table, norm_gain, w_q, w_kv, qk_gain, w_o, w_up, w_down, w_lat, w_conv, conv_bias):
    tokens = F * GH * GW
    positions = GH * GW
    onehot = (actions[:, None] == jnp.arange(ACTS, dtype=jnp.int32)[None, :]).astype(jnp.bfloat16)
    embedding = jnp.dot(onehot, action_table, preferred_element_type=jnp.float32)
    stream = (frames.astype(jnp.float32) + embedding[:, None, None, :]).astype(jnp.bfloat16)
    normed = root_scale(stream.astype(jnp.float32), norm_gain).astype(jnp.bfloat16)
    flat_normed = normed.reshape(tokens, D)
    key_value = jnp.dot(flat_normed, w_kv.reshape(D, 2 * HD), preferred_element_type=jnp.float32).astype(jnp.bfloat16)
    key_rows = root_scale(key_value[:, :HD].astype(jnp.float32), qk_gain[1]).astype(jnp.bfloat16)
    key_rows = lax.optimization_barrier(key_rows).reshape(F, positions, HD)
    value_rows = key_value[:, HD:].reshape(F, positions, HD)
    frame_ids = jnp.arange(F, dtype=jnp.int32)
    causal = frame_ids[:, None] >= frame_ids[None, :]
    score_scale = 1.0 / math.sqrt(HD)

    def one_head(head_weights):
        query = jnp.dot(flat_normed, head_weights, preferred_element_type=jnp.float32).astype(jnp.bfloat16)
        query = root_scale(query.astype(jnp.float32), qk_gain[0]).astype(jnp.bfloat16)
        query = lax.optimization_barrier(query).reshape(F, positions, HD)
        scores = jnp.einsum('tpd,spd->pts', query.astype(jnp.float32), key_rows.astype(jnp.float32)) * score_scale
        scores = jnp.where(causal[None, :, :], scores, -jnp.inf)
        row_max = lax.optimization_barrier(jnp.max(scores, axis=-1, keepdims=True))
        exponent = jnp.exp(scores - row_max)
        totals = lax.optimization_barrier(jnp.sum(exponent, axis=-1))
        weights = lax.optimization_barrier(exponent.astype(jnp.bfloat16)).astype(jnp.float32)
        mixed_values = jnp.einsum('pts,spd->tpd', weights, value_rows.astype(jnp.float32))
        return (mixed_values / jnp.transpose(totals)[:, :, None]).astype(jnp.bfloat16)
    head_weights = jnp.transpose(w_q.reshape(D, HEADS, HD), (1, 0, 2))
    attended = lax.map(one_head, head_weights)
    attended = jnp.transpose(attended, (1, 2, 0, 3)).reshape(tokens, D)
    group_heads = D // N_SPACE
    group_units = FF // N_SPACE

    def one_group(running_total, group_index):
        head_part = lax.dynamic_slice_in_dim(attended, group_index * group_heads, group_heads, 1)
        out_rows = lax.dynamic_slice_in_dim(w_o, group_index * group_heads, group_heads, 0)
        up_part = lax.dynamic_slice_in_dim(w_up, group_index * group_units, group_units, 1)
        down_rows = lax.dynamic_slice_in_dim(w_down, group_index * group_units, group_units, 0)
        hidden = jax.nn.gelu(jnp.dot(flat_normed, up_part, preferred_element_type=jnp.float32), approximate=True).astype(jnp.bfloat16)
        partial_sum = jnp.dot(head_part, out_rows, preferred_element_type=jnp.float32)
        partial_sum = partial_sum + jnp.dot(hidden, down_rows, preferred_element_type=jnp.float32)
        rounded = lax.optimization_barrier(partial_sum.astype(jnp.bfloat16))
        return (running_total + rounded.astype(jnp.float32), None)
    running_total = lax.scan(one_group, jnp.zeros((tokens, D), jnp.float32), jnp.arange(N_SPACE, dtype=jnp.int32))[0]
    block_out = (stream.reshape(tokens, D).astype(jnp.float32) + running_total).astype(jnp.bfloat16)
    latent = jax.nn.silu(jnp.dot(block_out, w_lat, preferred_element_type=jnp.float32)).astype(jnp.bfloat16)
    latent = latent.reshape(F, GH, GW, C)
    padded = jnp.pad(latent, ((0, 0), (0, 1), (0, 1), (0, 0)))
    center = padded[:, :-1, :-1]
    right_cells = padded[:, :-1, 1:]
    below_cells = padded[:, 1:, :-1]
    corner = padded[:, 1:, 1:]
    even_even = tap_product(center, w_conv[1, 1]) + conv_bias
    even_odd = tap_product(right_cells, w_conv[1, 0]) + tap_product(center, w_conv[1, 2]) + conv_bias
    odd_even = tap_product(below_cells, w_conv[0, 1]) + tap_product(center, w_conv[2, 1]) + conv_bias
    odd_odd = tap_product(corner, w_conv[0, 0]) + tap_product(below_cells, w_conv[0, 2]) + tap_product(right_cells, w_conv[2, 0]) + tap_product(center, w_conv[2, 2]) + conv_bias
    upper = jnp.stack([even_even, even_odd], axis=3)
    lower = jnp.stack([odd_even, odd_odd], axis=3)
    decoded = jnp.stack([upper, lower], axis=2).reshape(F, 2 * GH, 2 * GW, C)
    return decoded.astype(jnp.bfloat16)
```

```python
import functools
import math

import jax
import jax.numpy as jnp
from jax import lax
from jax.experimental import pallas as pl
from jax.experimental.pallas import tpu as pltpu
from jax.sharding import PartitionSpec as P

MESH = pl.DeviceIdType.MESH
EPS = 1e-06
MASKED = -1e30
F32 = jnp.float32
BF16 = jnp.bfloat16
KINDS = ("q", "kv", "up", "o", "down")
N_SEMS = 144
TOKENS = 128
SUMS = 4


def device(core, x, y, z):
    return ((y * 2 + x // 2) * 2 + core, z * 2 + x % 2)


class Weight:
    def __init__(self, src, dst, along_rows):
        self.src, self.dst, self.along_rows = src, dst, along_rows
        self.size = src.shape[1] if along_rows else src.shape[0]

    def cut(self, ref, start, length, shard=None, shards=1):
        start = pl.multiple_of(start, 128)
        if shard is None:
            across = slice(None)
        elif isinstance(shard, int):
            across = slice(shard * self.size, (shard + shards) * self.size)
        else:
            step = 128 if self.along_rows else 16
            across = pl.ds(pl.multiple_of(shard * self.size, step), shards * self.size)
        if self.along_rows:
            return ref.at[pl.ds(start, length), across]
        return ref.at[across, pl.ds(start, length)]

    def own(self):
        return self.cut(self.dst, 0, 2048, 0)

    def src_half(self, core):
        return self.cut(self.src, core * 1024, 1024)

    def pair_half(self, core):
        return self.cut(self.dst, core * 1024, 1024, 1)

    def src_piece(self, core, y, x_hi):
        return self.cut(self.src, (core * 8 + y * 2 + x_hi) * 128, 128)

    def piece(self, core, y, x):
        return self.cut(self.dst, (core * 8 + y * 2 + x // 2) * 128, 128, 2 + x % 2)

    def region(self, core, y):
        return self.cut(self.dst, (core * 8 + y * 2) * 128, 256, 2, 2)

    def half_region(self, core, y, x_hi):
        return self.cut(self.dst, (core * 8 + y * 2 + x_hi) * 128, 128, 2, 2)


def root_scale(values, gain):
    return values * lax.rsqrt(jnp.mean(values * values, axis=-1, keepdims=True) + EPS) * gain


def kernel(
    frames, actions, table, norm_gain, wq, wkv, qk_gain, wo, wup, wdown, wlat, wconv, bias,
    out,
    frames_v, wq_v, wkv_v, wup_v, wo_v, wdown_v, wlat_v, wconv_v,
    x_v, n_v, q_v, qr_v, kvt_v, kvr_v, kvt_f, kvg_v, kvf_v, qn_v, ao_f, ao_v, at_v, h_v, p_v, pr_v,
    lat_v, lb_v, send_sem, recv_sem, local_sem,
):
    t, s = lax.axis_index("tm"), lax.axis_index("space")
    core, x_hi, y = t % 2, (t // 2) % 2, t // 4
    x_lo, z = s % 2, s // 2
    x = x_hi * 2 + x_lo
    other = 1 - core

    def at(dc=0, dx=0, dy=0, dz=0):
        return device((core + dc) % 2, (x + dx) % 4, (y + dy) % 4, (z + dz) % 8)

    above, below = (t, (s + 15) % 16), (t, (s + 1) % 16)
    barrier = pltpu.get_barrier_semaphore()
    near = [at(dz=1), at(dz=7), at(dz=2), at(dz=6), at(dz=4), at(dx=1), at(dx=3)]
    for partner in near + [above, below]:
        pl.semaphore_signal(barrier, inc=1, device_id=partner, device_id_type=MESH)

    def greet(step, carry):
        pl.semaphore_signal(
            barrier, inc=1, device_id=((t + step) % 16, s), device_id_type=MESH
        )
        return carry

    lax.fori_loop(1, 16, greet, 0)

    count = {"sem": 0, "local": 0}
    sent = []

    def take():
        count["sem"] += 1
        return count["sem"] - 1

    def remote(index, src, dst, target):
        return pltpu.make_async_remote_copy(
            src_ref=src, dst_ref=dst, send_sem=send_sem.at[index], recv_sem=recv_sem.at[index],
            device_id=target, device_id_type=MESH,
        )

    def push(index, src, dst, target):
        copy = remote(index, src, dst, target)
        copy.start()
        sent.append(copy)

    def arrive(index, dst):
        remote(index, dst, dst, (t, s)).wait_recv()

    def local(src, dst):
        copy = pltpu.make_async_copy(src, dst, local_sem.at[count["local"]])
        count["local"] += 1
        copy.start()
        return copy

    frames_copy = local(frames, frames_v)
    weights = {
        "q": Weight(wq, wq_v, True),
        "kv": Weight(wkv, wkv_v, False),
        "up": Weight(wup, wup_v, True),
        "o": Weight(wo, wo_v, False),
        "down": Weight(wdown, wdown_v, False),
    }
    own_copy = {kind: local(weights[kind].src, weights[kind].own()) for kind in KINDS}
    wlat_copy = local(wlat, wlat_v)
    wconv_copy = local(wconv, wconv_v)

    pl.semaphore_wait(barrier, 24)

    sems = {}

    def far_start(kind):
        w = weights[kind]
        sems[kind, "z"] = take()
        push(sems[kind, "z"], w.src_piece(core, y, x_hi), w.piece(core, y, x), at(dz=4))

    def pair_start(kind):
        w = weights[kind]
        sems[kind, "pair"] = take()
        target = device(core, (x + 3 + 2 * core) % 4, y, z)
        push(sems[kind, "pair"], w.src_half(core), w.pair_half(core), target)

    def pair_share(kind):
        w = weights[kind]
        arrive(sems[kind, "pair"], w.pair_half(core))
        sems[kind, "pair_c"] = take()
        push(sems[kind, "pair_c"], w.pair_half(core), w.pair_half(core), at(dc=1))

    def pair_done(kind):
        arrive(sems[kind, "pair_c"], weights[kind].pair_half(other))

    def row_start(kind):
        w = weights[kind]
        mine = w.piece(core, y, x)
        arrive(sems[kind, "z"], mine)
        for dx in (1, 3, 2):
            sems[kind, "x", dx] = take()
            push(sems[kind, "x", dx], mine, mine, at(dx=dx))

    def column_start(kind):
        w = weights[kind]
        for dx in (1, 3, 2):
            arrive(sems[kind, "x", dx], w.piece(core, y, (x + 4 - dx) % 4))
        mine = w.region(core, y)
        for dy in (1, 3):
            sems[kind, "y", dy] = take()
            push(sems[kind, "y", dy], mine, mine, at(dy=dy))
        sems[kind, "c", 0] = take()
        push(sems[kind, "c", 0], mine, mine, at(dc=1))

    def column_relay(kind):
        w = weights[kind]
        for dy, piece in ((1, 0), (3, 1)):
            row = (y + 4 - dy) % 4
            got = w.region(core, row)
            arrive(sems[kind, "y", dy], got)
            half = w.half_region(core, row, piece)
            sems[kind, "y2", dy] = take()
            push(sems[kind, "y2", dy], half, half, at(dy=dy))
            sems[kind, "c", dy] = take()
            push(sems[kind, "c", dy], got, got, at(dc=1))

    def column_end(kind):
        w = weights[kind]
        row = (y + 2) % 4
        for dy, piece in ((1, 0), (3, 1)):
            half = w.half_region(core, row, piece)
            arrive(sems[kind, "y2", dy], half)
            sems[kind, "c2", dy] = take()
            push(sems[kind, "c2", dy], half, half, at(dc=1))

    def far_done(kind):
        w = weights[kind]
        for dy in (0, 1, 3):
            arrive(sems[kind, "c", dy], w.region(other, (y + 4 - dy) % 4))
        for dy, piece in ((1, 0), (3, 1)):
            arrive(sems[kind, "c2", dy], w.half_region(other, (y + 2) % 4, piece))

    for kind in ("q", "kv"):
        far_start(kind)
        pair_start(kind)

    frames_copy.wait()
    row = lax.broadcasted_iota(jnp.int32, (TOKENS, TOKENS), 0)
    col = lax.broadcasted_iota(jnp.int32, (TOKENS, TOKENS), 1)
    turn = (col == (row & 7) * 16 + (row >> 3)).astype(F32).astype(BF16)
    moved = jnp.dot(turn, frames_v[...], preferred_element_type=F32)
    ids = actions[...]
    embedding = jnp.zeros((8, 2048), F32)
    for action in range(8):
        embedding += jnp.where(ids == action, table[action : action + 1, :].astype(F32), 0.0)
    stream = moved.reshape(16, 8, 2048) + embedding[None]
    x_v[0:128, :] = stream.reshape(TOKENS, 2048).astype(BF16)

    routes = (
        (1, slice(0, 128), slice(128, 256)),
        (7, slice(0, 128), slice(256, 384)),
        (2, slice(0, 64), slice(384, 448)),
        (6, slice(64, 128), slice(448, 512)),
    )
    token_sems = [take() for _ in routes]
    for index, (dz, home, away) in zip(token_sems, routes):
        push(index, x_v.at[home], x_v.at[away], at(dz=dz))
    for kind in ("up", "o", "down"):
        far_start(kind)
        pair_start(kind)

    def norm_block(index, carry):
        rows = pl.ds(pl.multiple_of(index * 16, 16), 16)
        n_v[rows, :] = root_scale(x_v[rows, :].astype(F32), norm_gain[...]).astype(BF16)
        return carry

    for kind in ("q", "kv"):
        row_start(kind)
    lax.fori_loop(0, 8, norm_block, 0)
    for kind in ("q", "kv"):
        column_start(kind)
        pair_share(kind)
    for kind in ("q", "kv"):
        column_relay(kind)
    row_start("up")
    for kind in ("q", "kv"):
        column_end(kind)
    column_start("up")
    for index, (dz, home, away) in zip(token_sems, routes):
        arrive(index, x_v.at[away])
    lax.fori_loop(8, 32, norm_block, 0)

    for kind in ("q", "kv"):
        own_copy[kind].wait()
        pair_done(kind)
        far_done(kind)
    for half in range(2):
        rows = slice(half * 256, half * 256 + 256)
        q_v[rows, :] = jnp.dot(n_v[rows, :], wq_v[...], preferred_element_type=F32).astype(BF16)
    kvt_v[...] = lax.dot_general(
        wkv_v[...], n_v[...], (((1,), (1,)), ((), ())), preferred_element_type=F32
    ).astype(BF16)
    kv_sems = [take() for _ in routes]
    kv_columns = (slice(128, 256), slice(256, 384), slice(384, 512), slice(384, 512))
    for slot, (index, (dz, home, away)) in enumerate(zip(kv_sems, routes)):
        push(index, kvt_v.at[:, kv_columns[slot]], kvr_v.at[slot], at(dz=8 - dz))
    q_sems = [take() for _ in routes]
    q_columns = (slice(512, 1024), slice(1024, 1536), slice(1536, 2048), slice(1536, 2048))
    for slot, (index, (dz, home, away)) in enumerate(zip(q_sems, routes)):
        push(index, q_v.at[away], qr_v.at[home, q_columns[slot]], at(dz=8 - dz))
    qr_v[:, 0:512] = q_v[0:128, :]

    def up_tiles(shard):
        def tile(index, carry):
            columns = pl.ds(pl.multiple_of(shard * 512 + index * 256, 256), 256)
            hidden = jnp.dot(n_v[...], wup_v[:, columns], preferred_element_type=F32)
            h_v[:, columns] = jax.nn.gelu(hidden, approximate=True).astype(BF16)
            return carry

        lax.fori_loop(0, 2, tile, 0)

    row_start("o")
    column_relay("up")
    row_start("down")
    column_start("o")
    own_copy["up"].wait()
    up_tiles(0)

    for slot, index in enumerate(kv_sems):
        arrive(index, kvr_v.at[slot])
    later_half = lax.broadcasted_iota(jnp.int32, (8, TOKENS), 1) >= 64
    for index, (plane, block) in enumerate((
        (z, kvt_v[:, 0:128].astype(F32)),
        (z + 1, kvr_v[0].astype(F32)),
        (z + 7, kvr_v[1].astype(F32)),
        (z + 2, kvr_v[2].astype(F32)),
        (z + 6, kvr_v[3].astype(F32)),
    )):
        near_plane, far_plane = plane % 8, (plane + 4) % 8
        places = (
            near_plane * 2 + x_lo,
            near_plane * 2 + 1 - x_lo,
            far_plane * 2,
            far_plane * 2 + 1,
        )
        for shard, place in enumerate(places):
            rows = pl.ds(pl.multiple_of(place * 8, 8), 8)
            for part in range(2):
                found = block[shard * 16 + part * 8 : shard * 16 + part * 8 + 8, :]
                if index == 4:
                    found = jnp.where(later_half, found, kvt_f[part, rows, :])
                kvt_f[part, rows, :] = found
    keys = root_scale(jnp.transpose(kvt_f[0]), qk_gain[1:2, :])
    values = jnp.transpose(kvt_f[1])
    kvg_v[t] = jnp.concatenate([keys, values], axis=1).astype(BF16)
    gather_sem = count["sem"]
    count["sem"] += 15

    def gather_send(step, carry):
        @pl.when(t + step < 16)
        def _():
            remote(
                gather_sem + step - 1, kvg_v.at[t], kvg_v.at[t], ((t + step) % 16, s)
            ).start()

        return carry

    def gather_wait(step, carry):
        @pl.when(t - step >= 0)
        def _():
            arrive(gather_sem + step - 1, kvg_v.at[(t + 16 - step) % 16])

        return carry

    def gather_sent(step, carry):
        @pl.when(t + step < 16)
        def _():
            remote(
                gather_sem + step - 1, kvg_v.at[t], kvg_v.at[t], ((t + step) % 16, s)
            ).wait_send()

        return carry

    lax.fori_loop(1, 16, gather_send, 0)

    column_end("up")
    pair_share("up")
    column_relay("o")
    column_start("down")

    for index, (slot, (dz, home, away)) in zip(q_sems, enumerate(routes)):
        arrive(index, qr_v.at[home, q_columns[slot]])
    for head in range(16):
        query = root_scale(qr_v[:, head * 128 : head * 128 + 128].astype(F32), qk_gain[0:1, :])
        qn_v[:, head] = query.astype(BF16).astype(F32).reshape(16, 8, 128)
    lax.fori_loop(1, 16, gather_wait, 0)

    def widen(index, carry):
        @pl.when(index <= t)
        def _():
            kvf_v[index] = kvg_v[index].astype(F32).reshape(16, 8, 256)

        @pl.when(index > t)
        def _():
            kvf_v[index] = jnp.zeros((16, 8, 256), F32)

        return carry

    lax.fori_loop(0, 16, widen, 0)
    allowed = col <= t * 8 + (row & 7)
    score_scale = 1.0 / math.sqrt(128)

    def attend(place, carry):
        query = qn_v[place].reshape(128, 128).astype(BF16)
        pair = kvf_v[:, place].reshape(128, 256).astype(BF16)
        scores = lax.dot_general(
            query, pair[:, 0:128], (((1,), (1,)), ((), ())), preferred_element_type=F32
        ) * score_scale
        scores = jnp.where(allowed, scores, MASKED)
        exponent = jnp.exp(scores - jnp.max(scores, axis=-1, keepdims=True))
        exponent = jnp.where(allowed, exponent, 0.0)
        totals = jnp.sum(exponent, axis=-1, keepdims=True)
        mixed = jnp.dot(exponent.astype(BF16), pair[:, 128:256], preferred_element_type=F32)
        mixed = mixed / totals
        rows = pl.ds(pl.multiple_of(place * 8, 8), 8)
        for head in range(16):
            ao_f[rows, head * 128 : head * 128 + 128] = mixed[head * 8 : head * 8 + 8, :]
        return carry

    lax.fori_loop(0, 16, attend, 0, unroll=2)
    ao_v[...] = ao_f[...].astype(BF16)
    at_v[0:128, :] = ao_v[:, 0:512]
    at_sems = [take() for _ in routes]
    for slot, (index, (dz, home, away)) in enumerate(zip(at_sems, routes)):
        push(index, ao_v.at[home, q_columns[slot]], at_v.at[away], at(dz=dz))

    column_end("o")
    column_relay("down")
    pair_done("up")
    up_tiles(1)
    pair_share("o")
    pair_share("down")
    column_end("down")
    far_done("up")
    up_tiles(2)
    up_tiles(3)
    for index, (dz, home, away) in zip(at_sems, routes):
        arrive(index, at_v.at[away])
    for kind in ("o", "down"):
        own_copy[kind].wait()
        pair_done(kind)
        far_done(kind)

    width = 2048 // SUMS
    sum_sems = []
    pr_places = ((0, slice(0, 128)), (1, slice(0, 128)), (2, slice(0, 64)), (2, slice(64, 128)))
    for chunk in range(SUMS):
        columns = slice(chunk * width, chunk * width + width)
        for half in range(2):
            rows = slice(half * 256, half * 256 + 256)
            part = jnp.dot(at_v[rows, :], wo_v[:, columns], preferred_element_type=F32)
            part += jnp.dot(h_v[rows, :], wdown_v[:, columns], preferred_element_type=F32)
            p_v[rows, columns] = part.astype(BF16)
        indices = [take() for _ in routes]
        sum_sems.append(indices)
        for slot, (index, (dz, home, away)) in enumerate(zip(indices, routes)):
            lead, span = pr_places[slot]
            push(index, p_v.at[away, columns], pr_v.at[lead, span, columns], at(dz=8 - dz))
    wlat_copy.wait()
    latent = jnp.zeros((TOKENS, 512), F32)
    for chunk in range(SUMS):
        columns = slice(chunk * width, chunk * width + width)
        for slot, index in enumerate(sum_sems[chunk]):
            lead, span = pr_places[slot]
            arrive(index, pr_v.at[lead, span, columns])
        total = p_v[0:128, columns].astype(F32)
        for lead in range(3):
            total += pr_v[lead, :, columns].astype(F32)
        block = (x_v[0:128, columns].astype(F32) + total).astype(BF16)
        latent += jnp.dot(block, wlat_v[columns, :], preferred_element_type=F32)
    lat_v[...] = (latent / (1.0 + jnp.exp(-latent))).astype(BF16)
    halo_sem = take()
    push(halo_sem, lat_v, lb_v, above)

    wconv_copy.wait()
    zero_rows = jnp.zeros((8, 512), F32)

    def right_of(cells):
        wide = cells.astype(F32)
        return jnp.concatenate([wide[8:, :], zero_rows], axis=0).astype(BF16)

    def tap(cells, down, across):
        return jnp.dot(cells, wconv_v[down, across], preferred_element_type=F32)

    o_row = lax.broadcasted_iota(jnp.int32, (256, 256), 0)
    o_col = lax.broadcasted_iota(jnp.int32, (256, 256), 1)
    weave = (o_col == (o_row & 1) * 128 + ((o_row >> 1) & 15) * 8 + (o_row >> 5)).astype(F32)
    weave = weave.astype(BF16)

    def store(parity, even, odd):
        pair = jnp.concatenate([even + bias[...], odd + bias[...]], axis=0).astype(BF16)
        woven = jnp.dot(weave, pair, preferred_element_type=F32).astype(BF16)
        out[:, parity] = woven.reshape(8, 32, 512)

    center = lat_v[...]
    right = right_of(center)
    store(0, tap(center, 1, 1), tap(right, 1, 0) + tap(center, 1, 2))
    odd_even = tap(center, 2, 1)
    odd_odd = tap(right, 2, 0) + tap(center, 2, 2)
    arrive(halo_sem, lb_v)
    under = jnp.where(s < 15, lb_v[...].astype(F32), 0.0).astype(BF16)
    corner = right_of(under)
    store(1, odd_even + tap(under, 0, 1), odd_odd + tap(corner, 0, 0) + tap(under, 0, 2))

    for copy in sent:
        copy.wait_send()
    lax.fori_loop(1, 16, gather_sent, 0)


def per_device(
    frames, actions, action_table, norm_gain, w_q, w_kv, qk_gain, w_o, w_up, w_down, w_lat, w_conv,
    conv_bias,
):
    w_kv = jnp.transpose(w_kv, (1, 2, 0)).reshape(16, 2048)
    vmem, anywhere = pl.BlockSpec(memory_space=pltpu.VMEM), pl.BlockSpec(memory_space=pl.ANY)
    flops = 2 * 512 * 2048 * (512 * 2 + 64 + 2048 * 2) + 2 * 128 * 512 * (2048 + 9 * 512)
    return pl.pallas_call(
        kernel,
        out_shape=jax.ShapeDtypeStruct((8, 2, 32, 512), BF16),
        in_specs=[
            anywhere, vmem, vmem, vmem, anywhere, anywhere, vmem, anywhere, anywhere, anywhere,
            anywhere, anywhere, vmem,
        ],
        out_specs=vmem,
        scratch_shapes=[
            pltpu.VMEM((128, 2048), BF16),
            pltpu.VMEM((2048, 512), BF16),
            pltpu.VMEM((64, 2048), BF16),
            pltpu.VMEM((2048, 2048), BF16),
            pltpu.VMEM((512, 2048), BF16),
            pltpu.VMEM((2048, 2048), BF16),
            pltpu.VMEM((2048, 512), BF16),
            pltpu.VMEM((3, 3, 512, 512), BF16),
            pltpu.VMEM((512, 2048), BF16),
            pltpu.VMEM((512, 2048), BF16),
            pltpu.VMEM((512, 512), BF16),
            pltpu.VMEM((128, 2048), BF16),
            pltpu.VMEM((64, 512), BF16),
            pltpu.VMEM((4, 64, 128), BF16),
            pltpu.VMEM((2, 128, 128), F32),
            pltpu.VMEM((16, 128, 256), BF16),
            pltpu.VMEM((16, 16, 8, 256), F32),
            pltpu.VMEM((16, 16, 8, 128), F32),
            pltpu.VMEM((128, 2048), F32),
            pltpu.VMEM((128, 2048), BF16),
            pltpu.VMEM((512, 512), BF16),
            pltpu.VMEM((512, 2048), BF16),
            pltpu.VMEM((512, 2048), BF16),
            pltpu.VMEM((3, 128, 2048), BF16),
            pltpu.VMEM((128, 512), BF16),
            pltpu.VMEM((128, 512), BF16),
            pltpu.SemaphoreType.DMA((N_SEMS,)),
            pltpu.SemaphoreType.DMA((N_SEMS,)),
            pltpu.SemaphoreType.DMA((8,)),
        ],
        compiler_params=pltpu.CompilerParams(
            collective_id=1, has_side_effects=True, vmem_limit_bytes=60 * 1024 * 1024
        ),
        cost_estimate=pl.CostEstimate(flops=flops, bytes_accessed=14000000, transcendentals=0),
        name="block",
    )(
        frames.reshape(128, 2048),
        actions.reshape(8, 1),
        action_table,
        norm_gain.reshape(1, 2048),
        w_q,
        w_kv,
        qk_gain,
        w_o,
        w_up,
        w_down,
        w_lat,
        w_conv,
        conv_bias.reshape(1, 512),
    )


def solution(mesh):
    return jax.shard_map(
        per_device,
        mesh=mesh,
        in_specs=(
            P("tm", "space", None, None),
            P("tm"),
            P(),
            P(),
            P(None, "space"),
            P(None, None, "space"),
            P(),
            P("space", None),
            P(None, "space"),
            P("space", None),
            P(),
            P(),
            P(),
        ),
        out_specs=P("tm", "space", None, None),
        check_vma=False,
    )
```

```python
import functools
import math

import jax
import jax.numpy as jnp
from jax import lax
from jax.experimental import pallas as pl
from jax.experimental.pallas import tpu as pltpu
from jax.sharding import PartitionSpec as P

MESH = pl.DeviceIdType.MESH
EPS = 1e-06
MASKED = -1e30
F32 = jnp.float32
BF16 = jnp.bfloat16
KINDS = ("q", "kv", "up", "o", "down")
N_SEMS = 144
TOKENS = 128
SUMS = 4


def device(core, x, y, z):
    return ((y * 2 + x // 2) * 2 + core, z * 2 + x % 2)


class Weight:
    def __init__(self, src, dst, along_rows):
        self.src, self.dst, self.along_rows = src, dst, along_rows
        self.size = src.shape[1] if along_rows else src.shape[0]

    def cut(self, ref, start, length, shard=None, shards=1):
        start = pl.multiple_of(start, 128)
        if shard is None:
            across = slice(None)
        elif isinstance(shard, int):
            across = slice(shard * self.size, (shard + shards) * self.size)
        else:
            step = 128 if self.along_rows else 16
            across = pl.ds(pl.multiple_of(shard * self.size, step), shards * self.size)
        if self.along_rows:
            return ref.at[pl.ds(start, length), across]
        return ref.at[across, pl.ds(start, length)]

    def own(self):
        return self.cut(self.dst, 0, 2048, 0)

    def src_half(self, core):
        return self.cut(self.src, core * 1024, 1024)

    def pair_half(self, core):
        return self.cut(self.dst, core * 1024, 1024, 1)

    def src_piece(self, core, y, x_hi):
        return self.cut(self.src, (core * 8 + y * 2 + x_hi) * 128, 128)

    def piece(self, core, y, x):
        return self.cut(self.dst, (core * 8 + y * 2 + x // 2) * 128, 128, 2 + x % 2)

    def region(self, core, y):
        return self.cut(self.dst, (core * 8 + y * 2) * 128, 256, 2, 2)

    def half_region(self, core, y, x_hi):
        return self.cut(self.dst, (core * 8 + y * 2 + x_hi) * 128, 128, 2, 2)


def root_scale(values, gain):
    return values * lax.rsqrt(jnp.mean(values * values, axis=-1, keepdims=True) + EPS) * gain


def kernel(
    frames, actions, table, norm_gain, wq, wkv, qk_gain, wo, wup, wdown, wlat, wconv, bias,
    out,
    frames_v, wq_v, wkv_v, wup_v, wo_v, wdown_v, wlat_v, wconv_v,
    x_v, n_v, q_v, qr_v, kvt_v, kvr_v, kvt_f, kvg_v, kvf_v, qn_v, ao_f, ao_v, at_v, h_v, p_v, pm_v, pr_v,
    lat_v, lb_v, send_sem, recv_sem, local_sem,
):
    t, s = lax.axis_index("tm"), lax.axis_index("space")
    core, x_hi, y = t % 2, (t // 2) % 2, t // 4
    x_lo, z = s % 2, s // 2
    x = x_hi * 2 + x_lo
    other = 1 - core

    def at(dc=0, dx=0, dy=0, dz=0):
        return device((core + dc) % 2, (x + dx) % 4, (y + dy) % 4, (z + dz) % 8)

    above, below = (t, (s + 15) % 16), (t, (s + 1) % 16)
    barrier = pltpu.get_barrier_semaphore()
    near = [at(dz=1), at(dz=7), at(dz=2), at(dz=6), at(dz=4), at(dx=1), at(dx=3)]
    for partner in near + [above, below, at(dc=1)]:
        pl.semaphore_signal(barrier, inc=1, device_id=partner, device_id_type=MESH)

    def greet(step, carry):
        pl.semaphore_signal(
            barrier, inc=1, device_id=((t + 2 * step) % 16, s), device_id_type=MESH
        )
        return carry

    lax.fori_loop(1, 8, greet, 0)

    count = {"sem": 0, "local": 0}
    sent = []

    def take():
        count["sem"] += 1
        return count["sem"] - 1

    def remote(index, src, dst, target):
        return pltpu.make_async_remote_copy(
            src_ref=src, dst_ref=dst, send_sem=send_sem.at[index], recv_sem=recv_sem.at[index],
            device_id=target, device_id_type=MESH,
        )

    def push(index, src, dst, target):
        copy = remote(index, src, dst, target)
        copy.start()
        sent.append(copy)

    def arrive(index, dst):
        remote(index, dst, dst, (t, s)).wait_recv()

    def local(src, dst):
        copy = pltpu.make_async_copy(src, dst, local_sem.at[count["local"]])
        count["local"] += 1
        copy.start()
        return copy

    frames_copy = local(frames, frames_v)
    weights = {
        "q": Weight(wq, wq_v, True),
        "kv": Weight(wkv, wkv_v, False),
        "up": Weight(wup, wup_v, True),
        "o": Weight(wo, wo_v, False),
        "down": Weight(wdown, wdown_v, False),
    }
    own_copy = {kind: local(weights[kind].src, weights[kind].own()) for kind in KINDS}
    wlat_copy = local(wlat, wlat_v)
    wconv_copy = local(wconv, wconv_v)

    pl.semaphore_wait(barrier, 17)

    sems = {}

    def far_start(kind):
        w = weights[kind]
        sems[kind, "z"] = take()
        push(sems[kind, "z"], w.src_piece(core, y, x_hi), w.piece(core, y, x), at(dz=4))

    def pair_start(kind):
        w = weights[kind]
        sems[kind, "pair"] = take()
        target = device(core, (x + 3 + 2 * core) % 4, y, z)
        push(sems[kind, "pair"], w.src_half(core), w.pair_half(core), target)

    def pair_share(kind):
        w = weights[kind]
        arrive(sems[kind, "pair"], w.pair_half(core))
        sems[kind, "pair_c"] = take()
        push(sems[kind, "pair_c"], w.pair_half(core), w.pair_half(core), at(dc=1))

    def pair_done(kind):
        arrive(sems[kind, "pair_c"], weights[kind].pair_half(other))

    def row_start(kind):
        w = weights[kind]
        mine = w.piece(core, y, x)
        arrive(sems[kind, "z"], mine)
        for dx in (1, 3, 2):
            sems[kind, "x", dx] = take()
            push(sems[kind, "x", dx], mine, mine, at(dx=dx))

    def column_start(kind):
        w = weights[kind]
        for dx in (1, 3, 2):
            arrive(sems[kind, "x", dx], w.piece(core, y, (x + 4 - dx) % 4))
        mine = w.region(core, y)
        for dy in (1, 3):
            sems[kind, "y", dy] = take()
            push(sems[kind, "y", dy], mine, mine, at(dy=dy))
        sems[kind, "c", 0] = take()
        push(sems[kind, "c", 0], mine, mine, at(dc=1))

    def column_relay(kind):
        w = weights[kind]
        for dy, piece in ((1, 0), (3, 1)):
            row = (y + 4 - dy) % 4
            got = w.region(core, row)
            arrive(sems[kind, "y", dy], got)
            half = w.half_region(core, row, piece)
            sems[kind, "y2", dy] = take()
            push(sems[kind, "y2", dy], half, half, at(dy=dy))
            sems[kind, "c", dy] = take()
            push(sems[kind, "c", dy], got, got, at(dc=1))

    def column_end(kind):
        w = weights[kind]
        row = (y + 2) % 4
        for dy, piece in ((1, 0), (3, 1)):
            half = w.half_region(core, row, piece)
            arrive(sems[kind, "y2", dy], half)
            sems[kind, "c2", dy] = take()
            push(sems[kind, "c2", dy], half, half, at(dc=1))

    def far_done(kind):
        w = weights[kind]
        for dy in (0, 1, 3):
            arrive(sems[kind, "c", dy], w.region(other, (y + 4 - dy) % 4))
        for dy, piece in ((1, 0), (3, 1)):
            arrive(sems[kind, "c2", dy], w.half_region(other, (y + 2) % 4, piece))

    for kind in ("q", "kv", "up"):
        far_start(kind)
    for kind in ("q", "kv"):
        pair_start(kind)

    frames_copy.wait()
    row = lax.broadcasted_iota(jnp.int32, (TOKENS, TOKENS), 0)
    col = lax.broadcasted_iota(jnp.int32, (TOKENS, TOKENS), 1)
    turn = (col == (row & 7) * 16 + (row >> 3)).astype(F32).astype(BF16)
    moved = jnp.dot(turn, frames_v[...], preferred_element_type=F32)
    frame_row = lax.broadcasted_iota(jnp.int32, (8, 2048), 0)
    ids = jnp.zeros((8, 2048), jnp.int32)
    for frame in range(8):
        ids = jnp.where(frame_row == frame, actions[frame], ids)
    embedding = jnp.zeros((8, 2048), F32)
    for action in range(8):
        embedding += jnp.where(ids == action, table[action : action + 1, :].astype(F32), 0.0)
    stream = moved.reshape(16, 8, 2048) + embedding[None]
    x_v[0:128, :] = stream.reshape(TOKENS, 2048).astype(BF16)

    token_sems = {}

    def token_send(name, home, away, dz):
        token_sems[name] = take()
        push(token_sems[name], x_v.at[home], x_v.at[away], at(dz=dz))

    token_send("up first", slice(0, 64), slice(128, 192), 1)
    token_send("down last", slice(64, 128), slice(320, 384), 7)
    token_send("up last", slice(64, 128), slice(192, 256), 1)
    token_send("down first", slice(0, 64), slice(256, 320), 7)

    def token_arrive(name, away):
        arrive(token_sems[name], x_v.at[away])

    def norm_rows(first, last):
        def block(index, carry):
            rows = pl.ds(pl.multiple_of(index * 16, 16), 16)
            n_v[rows, :] = root_scale(x_v[rows, :].astype(F32), norm_gain[...]).astype(BF16)
            return carry

        lax.fori_loop(first // 16, last // 16, block, 0)

    for kind in ("q", "kv"):
        row_start(kind)
    norm_rows(0, 128)
    row_start("up")
    for kind in ("o", "down"):
        far_start(kind)
    for kind in ("q", "kv"):
        column_start(kind)
    pair_start("up")
    token_arrive("up first", slice(128, 192))
    token_send("up on", slice(128, 192), slice(384, 448), 1)
    token_arrive("down last", slice(320, 384))
    token_send("down on", slice(320, 384), slice(448, 512), 7)
    column_start("up")
    for kind in ("q", "kv"):
        pair_share(kind)
        column_relay(kind)
    for kind in ("q", "kv"):
        column_end(kind)
    token_arrive("up last", slice(192, 256))
    token_arrive("down first", slice(256, 320))
    norm_rows(128, 384)
    row_start("o")
    row_start("down")
    for kind in ("o", "down"):
        pair_start(kind)
    token_arrive("up on", slice(384, 448))
    token_arrive("down on", slice(448, 512))
    norm_rows(384, 512)

    for kind in ("q", "kv"):
        own_copy[kind].wait()
        pair_done(kind)
        far_done(kind)
    routes = (
        (1, slice(0, 128), slice(128, 256)),
        (7, slice(0, 128), slice(256, 384)),
        (2, slice(0, 64), slice(384, 448)),
        (6, slice(64, 128), slice(448, 512)),
    )
    kvt_v[...] = lax.dot_general(
        wkv_v[...], n_v[...], (((1,), (1,)), ((), ())), preferred_element_type=F32
    ).astype(BF16)
    kv_sems = [take() for _ in routes]
    kv_columns = (slice(128, 256), slice(256, 384), slice(384, 512), slice(384, 512))
    for slot, (index, (dz, home, away)) in enumerate(zip(kv_sems, routes)):
        push(index, kvt_v.at[:, kv_columns[slot]], kvr_v.at[slot], at(dz=8 - dz))
    for half in range(2):
        rows = slice(half * 256, half * 256 + 256)
        q_v[rows, :] = jnp.dot(n_v[rows, :], wq_v[...], preferred_element_type=F32).astype(BF16)
    q_sems = [take() for _ in routes]
    q_columns = (slice(512, 1024), slice(1024, 1536), slice(1536, 2048), slice(1536, 2048))
    for slot, (index, (dz, home, away)) in enumerate(zip(q_sems, routes)):
        push(index, q_v.at[away], qr_v.at[home, q_columns[slot]], at(dz=8 - dz))
    qr_v[:, 0:512] = q_v[0:128, :]

    def up_tiles(shard):
        def tile(index, carry):
            columns = pl.ds(pl.multiple_of(shard * 512 + index * 256, 256), 256)
            hidden = jnp.dot(n_v[...], wup_v[:, columns], preferred_element_type=F32)
            h_v[:, columns] = jax.nn.gelu(hidden, approximate=True).astype(BF16)
            return carry

        lax.fori_loop(0, 2, tile, 0)

    column_start("o")
    column_relay("up")
    column_start("down")
    own_copy["up"].wait()
    up_tiles(0)

    for slot, index in enumerate(kv_sems):
        arrive(index, kvr_v.at[slot])
    later_half = lax.broadcasted_iota(jnp.int32, (8, TOKENS), 1) >= 64
    for index, (plane, block) in enumerate((
        (z, kvt_v[:, 0:128].astype(F32)),
        (z + 1, kvr_v[0].astype(F32)),
        (z + 7, kvr_v[1].astype(F32)),
        (z + 2, kvr_v[2].astype(F32)),
        (z + 6, kvr_v[3].astype(F32)),
    )):
        near_plane, far_plane = plane % 8, (plane + 4) % 8
        places = (
            near_plane * 2 + x_lo,
            near_plane * 2 + 1 - x_lo,
            far_plane * 2,
            far_plane * 2 + 1,
        )
        for shard, place in enumerate(places):
            rows = pl.ds(pl.multiple_of(place * 8, 8), 8)
            for part in range(2):
                found = block[shard * 16 + part * 8 : shard * 16 + part * 8 + 8, :]
                if index == 4:
                    found = jnp.where(later_half, found, kvt_f[part, rows, :])
                kvt_f[part, rows, :] = found
    keys = root_scale(jnp.transpose(kvt_f[0]), qk_gain[1:2, :])
    values = jnp.transpose(kvt_f[1])
    kvg_v[t] = jnp.concatenate([keys, values], axis=1).astype(BF16)
    chip = t // 2
    gather_sem, share_sem = count["sem"], count["sem"] + 7
    count["sem"] += 15

    def gather(step):
        mine = kvg_v.at[t]
        return remote(gather_sem + step - 1, mine, mine, ((t + 2 * step) % 16, s))

    def share(step):
        got = kvg_v.at[(t + 16 - 2 * step) % 16]
        return remote(share_sem + step, got, got, at(dc=1))

    def gather_send(step, carry):
        @pl.when(chip + step < 8)
        def _():
            gather(step).start()

        return carry

    def gather_pass(step, carry):
        @pl.when(chip - step >= 0)
        def _():
            arrive(gather_sem + step - 1, kvg_v.at[(t + 16 - 2 * step) % 16])
            share(step).start()

        return carry

    def gather_wait(step, carry):
        @pl.when(chip - step >= 0)
        def _():
            arrive(share_sem + step, kvg_v.at[(t + 16 - 2 * step + 1 - 2 * core) % 16])

        return carry

    def gather_sent(step, carry):
        @pl.when(chip + step < 8)
        def _():
            gather(step).wait_send()

        @pl.when(chip - step >= 0)
        def _():
            share(step).wait_send()

        return carry

    lax.fori_loop(1, 8, gather_send, 0)

    @pl.when(core == 0)
    def _():
        share(0).start()

    column_end("up")
    pair_share("up")
    column_relay("o")
    pair_done("up")
    up_tiles(1)
    column_relay("down")

    for index, (slot, (dz, home, away)) in zip(q_sems, enumerate(routes)):
        arrive(index, qr_v.at[home, q_columns[slot]])
    for head in range(16):
        query = root_scale(qr_v[:, head * 128 : head * 128 + 128].astype(F32), qk_gain[0:1, :])
        qn_v[:, head] = query.astype(BF16).astype(F32).reshape(16, 8, 128)
    lax.fori_loop(1, 8, gather_pass, 0)

    @pl.when(core == 1)
    def _():
        arrive(share_sem, kvg_v.at[t - 1])

    lax.fori_loop(1, 8, gather_wait, 0)

    def widen(index, carry):
        @pl.when(index <= t)
        def _():
            kvf_v[index] = kvg_v[index].astype(F32).reshape(16, 8, 256)

        @pl.when(index > t)
        def _():
            kvf_v[index] = jnp.zeros((16, 8, 256), F32)

        return carry

    lax.fori_loop(0, 16, widen, 0)
    allowed = col <= t * 8 + (row & 7)
    score_scale = 1.0 / math.sqrt(128)

    def attend(place, carry):
        query = qn_v[place].reshape(128, 128).astype(BF16)
        pair = kvf_v[:, place].reshape(128, 256).astype(BF16)
        scores = lax.dot_general(
            query, pair[:, 0:128], (((1,), (1,)), ((), ())), preferred_element_type=F32
        ) * score_scale
        scores = jnp.where(allowed, scores, MASKED)
        exponent = jnp.exp(scores - jnp.max(scores, axis=-1, keepdims=True))
        exponent = jnp.where(allowed, exponent, 0.0)
        totals = jnp.sum(exponent, axis=-1, keepdims=True)
        mixed = jnp.dot(exponent.astype(BF16), pair[:, 128:256], preferred_element_type=F32)
        mixed = mixed / totals
        rows = pl.ds(pl.multiple_of(place * 8, 8), 8)
        for head in range(16):
            ao_f[rows, head * 128 : head * 128 + 128] = mixed[head * 8 : head * 8 + 8, :]
        return carry

    lax.fori_loop(0, 16, attend, 0, unroll=2)
    ao_v[...] = ao_f[...].astype(BF16)
    at_v[0:128, :] = ao_v[:, 0:512]
    at_sems = [take() for _ in routes]
    for slot, (index, (dz, home, away)) in enumerate(zip(at_sems, routes)):
        push(index, ao_v.at[home, q_columns[slot]], at_v.at[away], at(dz=dz))
    pair_share("o")
    pair_share("down")
    column_end("o")
    column_end("down")
    far_done("up")
    up_tiles(2)
    up_tiles(3)
    for index, (dz, home, away) in zip(at_sems, routes):
        arrive(index, at_v.at[away])
    for kind in ("o", "down"):
        own_copy[kind].wait()
        pair_done(kind)
        far_done(kind)

    width = 2048 // SUMS
    half_sems, sum_sems = [], []
    merges = ((7, slice(384, 448), slice(128, 192)), (1, slice(448, 512), slice(320, 384)))

    def chunk_of(chunk):
        return slice(chunk * width, chunk * width + width)

    def multiply(chunk):
        columns = chunk_of(chunk)
        for half in (1, 0):
            rows = slice(half * 256, half * 256 + 256)
            part = jnp.dot(at_v[rows, :], wo_v[:, columns], preferred_element_type=F32)
            part += jnp.dot(h_v[rows, :], wdown_v[:, columns], preferred_element_type=F32)
            p_v[rows, columns] = part.astype(BF16)
        indices = [take() for _ in merges]
        half_sems.append(indices)
        for side, (index, (dz, away, near_rows)) in enumerate(zip(indices, merges)):
            push(index, p_v.at[away, columns], pm_v.at[side, :, columns], at(dz=dz))

    def merge(chunk):
        columns = chunk_of(chunk)
        for side, (dz, away, near_rows) in enumerate(merges):
            arrive(half_sems[chunk][side], pm_v.at[side, :, columns])
            both = p_v[near_rows, columns].astype(F32) + pm_v[side, :, columns].astype(F32)
            p_v[near_rows, columns] = both.astype(BF16)
        indices = [take() for _ in range(2)]
        sum_sems.append(indices)
        for side, (dz, rows) in enumerate(((7, slice(128, 256)), (1, slice(256, 384)))):
            push(indices[side], p_v.at[rows, columns], pr_v.at[side, :, columns], at(dz=dz))

    multiply(0)
    for chunk in range(1, SUMS):
        multiply(chunk)
        merge(chunk - 1)
    merge(SUMS - 1)
    wlat_copy.wait()
    latent = jnp.zeros((TOKENS, 512), F32)
    for chunk in range(SUMS):
        columns = chunk_of(chunk)
        total = p_v[0:128, columns].astype(F32)
        for side in range(2):
            arrive(sum_sems[chunk][side], pr_v.at[side, :, columns])
            total += pr_v[side, :, columns].astype(F32)
        block = (x_v[0:128, columns].astype(F32) + total).astype(BF16)
        latent += jnp.dot(block, wlat_v[columns, :], preferred_element_type=F32)
    lat_v[...] = (latent / (1.0 + jnp.exp(-latent))).astype(BF16)
    halo_sem = take()
    push(halo_sem, lat_v, lb_v, above)

    wconv_copy.wait()
    zero_rows = jnp.zeros((8, 512), F32)

    def right_of(cells):
        wide = cells.astype(F32)
        return jnp.concatenate([wide[8:, :], zero_rows], axis=0).astype(BF16)

    def tap(cells, down, across):
        return jnp.dot(cells, wconv_v[down, across], preferred_element_type=F32)

    o_row = lax.broadcasted_iota(jnp.int32, (256, 256), 0)
    o_col = lax.broadcasted_iota(jnp.int32, (256, 256), 1)
    weave = (o_col == (o_row & 1) * 128 + ((o_row >> 1) & 15) * 8 + (o_row >> 5)).astype(F32)
    weave = weave.astype(BF16)

    def store(parity, even, odd):
        pair = jnp.concatenate([even + bias[...], odd + bias[...]], axis=0).astype(BF16)
        woven = jnp.dot(weave, pair, preferred_element_type=F32).astype(BF16)
        out[:, parity] = woven.reshape(8, 32, 512)

    center = lat_v[...]
    right = right_of(center)
    store(0, tap(center, 1, 1), tap(right, 1, 0) + tap(center, 1, 2))
    odd_even = tap(center, 2, 1)
    odd_odd = tap(right, 2, 0) + tap(center, 2, 2)
    arrive(halo_sem, lb_v)
    under = jnp.where(s < 15, lb_v[...].astype(F32), 0.0).astype(BF16)
    corner = right_of(under)
    store(1, odd_even + tap(under, 0, 1), odd_odd + tap(corner, 0, 0) + tap(under, 0, 2))

    for copy in sent:
        copy.wait_send()

    @pl.when(core == 0)
    def _():
        share(0).wait_send()

    lax.fori_loop(1, 8, gather_sent, 0)


def per_device(
    frames, actions, action_table, norm_gain, w_q, w_kv, qk_gain, w_o, w_up, w_down, w_lat, w_conv,
    conv_bias,
):
    w_kv = jnp.transpose(w_kv, (1, 2, 0)).reshape(16, 2048)
    vmem, anywhere = pl.BlockSpec(memory_space=pltpu.VMEM), pl.BlockSpec(memory_space=pl.ANY)
    smem = pl.BlockSpec(memory_space=pltpu.SMEM)
    flops = 2 * 512 * 2048 * (512 * 2 + 64 + 2048 * 2) + 2 * 128 * 512 * (2048 + 9 * 512)
    return pl.pallas_call(
        kernel,
        out_shape=jax.ShapeDtypeStruct((8, 2, 32, 512), BF16),
        in_specs=[
            anywhere, smem, vmem, vmem, anywhere, anywhere, vmem, anywhere, anywhere, anywhere,
            anywhere, anywhere, vmem,
        ],
        out_specs=vmem,
        scratch_shapes=[
            pltpu.VMEM((128, 2048), BF16),
            pltpu.VMEM((2048, 512), BF16),
            pltpu.VMEM((64, 2048), BF16),
            pltpu.VMEM((2048, 2048), BF16),
            pltpu.VMEM((512, 2048), BF16),
            pltpu.VMEM((2048, 2048), BF16),
            pltpu.VMEM((2048, 512), BF16),
            pltpu.VMEM((3, 3, 512, 512), BF16),
            pltpu.VMEM((512, 2048), BF16),
            pltpu.VMEM((512, 2048), BF16),
            pltpu.VMEM((512, 512), BF16),
            pltpu.VMEM((128, 2048), BF16),
            pltpu.VMEM((64, 512), BF16),
            pltpu.VMEM((4, 64, 128), BF16),
            pltpu.VMEM((2, 128, 128), F32),
            pltpu.VMEM((16, 128, 256), BF16),
            pltpu.VMEM((16, 16, 8, 256), F32),
            pltpu.VMEM((16, 16, 8, 128), F32),
            pltpu.VMEM((128, 2048), F32),
            pltpu.VMEM((128, 2048), BF16),
            pltpu.VMEM((512, 512), BF16),
            pltpu.VMEM((512, 2048), BF16),
            pltpu.VMEM((512, 2048), BF16),
            pltpu.VMEM((2, 64, 2048), BF16),
            pltpu.VMEM((2, 128, 2048), BF16),
            pltpu.VMEM((128, 512), BF16),
            pltpu.VMEM((128, 512), BF16),
            pltpu.SemaphoreType.DMA((N_SEMS,)),
            pltpu.SemaphoreType.DMA((N_SEMS,)),
            pltpu.SemaphoreType.DMA((8,)),
        ],
        compiler_params=pltpu.CompilerParams(
            collective_id=1, has_side_effects=True, vmem_limit_bytes=60 * 1024 * 1024
        ),
        cost_estimate=pl.CostEstimate(flops=flops, bytes_accessed=14000000, transcendentals=0),
        name="block",
    )(
        frames.reshape(128, 2048),
        actions,
        action_table,
        norm_gain.reshape(1, 2048),
        w_q,
        w_kv,
        qk_gain,
        w_o,
        w_up,
        w_down,
        w_lat,
        w_conv,
        conv_bias.reshape(1, 512),
    )


def solution(mesh):
    return jax.shard_map(
        per_device,
        mesh=mesh,
        in_specs=(
            P("tm", "space", None, None),
            P("tm"),
            P(),
            P(),
            P(None, "space"),
            P(None, None, "space"),
            P(),
            P("space", None),
            P(None, "space"),
            P("space", None),
            P(),
            P(),
            P(),
        ),
        out_specs=P("tm", "space", None, None),
        check_vma=False,
    )
```

```python
import functools
import math

import jax
import jax.numpy as jnp
from jax import lax
from jax.experimental import pallas as pl
from jax.experimental.pallas import tpu as pltpu
from jax.sharding import PartitionSpec as P

MESH = pl.DeviceIdType.MESH
EPS = 1e-06
MASKED = -1e30
F32 = jnp.float32
BF16 = jnp.bfloat16
KINDS = ("q", "kv", "up", "od")
N_SEMS = 112
TOKENS = 128


def device(core, x, y, z):
    return ((y * 2 + x // 2) * 2 + core, z * 2 + x % 2)


class Weight:
    def __init__(self, src, dst, along_rows):
        self.src, self.dst, self.along_rows = src, dst, along_rows
        self.size = src.shape[1] if along_rows else src.shape[0]

    def cut(self, ref, start, length, shard=None, shards=1):
        start = pl.multiple_of(start, 128)
        if shard is None:
            across = slice(None)
        elif isinstance(shard, int):
            across = slice(shard * self.size, (shard + shards) * self.size)
        else:
            step = 128 if self.along_rows else 16
            across = pl.ds(pl.multiple_of(shard * self.size, step), shards * self.size)
        if self.along_rows:
            return ref.at[pl.ds(start, length), across]
        return ref.at[across, pl.ds(start, length)]

    def own(self):
        return self.cut(self.dst, 0, 2048, 0)

    def src_half(self, core):
        return self.cut(self.src, core * 1024, 1024)

    def pair_half(self, core):
        return self.cut(self.dst, core * 1024, 1024, 1)

    def src_piece(self, core, y, x_hi):
        return self.cut(self.src, (core * 8 + y * 2 + x_hi) * 128, 128)

    def piece(self, core, y, x):
        return self.cut(self.dst, (core * 8 + y * 2 + x // 2) * 128, 128, 2 + x % 2)

    def region(self, core, y):
        return self.cut(self.dst, (core * 8 + y * 2) * 128, 256, 2, 2)

    def half_region(self, core, y, x_hi):
        return self.cut(self.dst, (core * 8 + y * 2 + x_hi) * 128, 128, 2, 2)


class Folded(Weight):
    def __init__(self, src, dst):
        self.src, self.dst = src, dst

    def own(self):
        return self.dst.at[0]

    def src_half(self, core):
        return self.src.at[pl.ds(pl.multiple_of(core * 320, 320), 320)]

    def pair_half(self, core):
        return self.dst.at[1, pl.ds(pl.multiple_of(core * 320, 320), 320)]

    def block(self, core, y):
        rows = pl.ds(pl.multiple_of((core * 2 + y // 2) * 160, 160), 160)
        return rows, (y % 2) * 256

    def src_piece(self, core, y, x_hi):
        rows, column = self.block(core, y)
        return self.src.at[rows, pl.ds(pl.multiple_of(column + x_hi * 128, 128), 128)]

    def piece(self, core, y, x):
        rows, column = self.block(core, y)
        columns = pl.ds(pl.multiple_of(column + x // 2 * 128, 128), 128)
        return self.dst.at[2 + x % 2, rows, columns]

    def region(self, core, y):
        rows, column = self.block(core, y)
        return self.dst.at[2:4, rows, pl.ds(pl.multiple_of(column, 256), 256)]

    def half_region(self, core, y, x_hi):
        rows, column = self.block(core, y)
        return self.dst.at[2:4, rows, pl.ds(pl.multiple_of(column + x_hi * 128, 128), 128)]


def root_scale(values, gain):
    return values * lax.rsqrt(jnp.mean(values * values, axis=-1, keepdims=True) + EPS) * gain


def kernel(
    frames, actions, table, norm_gain, wq, wkv, qk_gain, wo, wup, wdown, wlat, wconv, bias,
    out,
    frames_v, wq_v, wkv_v, wup_v, wo_v, wdown_v, wlat_v, wconv_v, od_v, ods_v,
    x_v, n_v, q_v, qr_v, kvt_v, kvr_v, kvt_f, kvg_v, kvf_v, qn_v, ao_f, ao_v, at_v, h_v, p_v, pr_v, ffn_f,
    lat_v, lb_v, send_sem, recv_sem, local_sem,
):
    t, s = lax.axis_index("tm"), lax.axis_index("space")
    core, x_hi, y = t % 2, (t // 2) % 2, t // 4
    x_lo, z = s % 2, s // 2
    x = x_hi * 2 + x_lo
    other = 1 - core

    def at(dc=0, dx=0, dy=0, dz=0):
        return device((core + dc) % 2, (x + dx) % 4, (y + dy) % 4, (z + dz) % 8)

    above, below = (t, (s + 15) % 16), (t, (s + 1) % 16)
    barrier = pltpu.get_barrier_semaphore()
    near = [at(dz=1), at(dz=7), at(dz=2), at(dz=6), at(dz=4), at(dx=1), at(dx=3)]
    for partner in near + [above, below, at(dc=1)]:
        pl.semaphore_signal(barrier, inc=1, device_id=partner, device_id_type=MESH)

    def greet(step, carry):
        pl.semaphore_signal(
            barrier, inc=1, device_id=((t + 2 * step) % 16, s), device_id_type=MESH
        )
        return carry

    lax.fori_loop(1, 8, greet, 0)

    count = {"sem": 0, "local": 0}
    sent = []

    def take():
        count["sem"] += 1
        return count["sem"] - 1

    def remote(index, src, dst, target):
        return pltpu.make_async_remote_copy(
            src_ref=src, dst_ref=dst, send_sem=send_sem.at[index], recv_sem=recv_sem.at[index],
            device_id=target, device_id_type=MESH,
        )

    def push(index, src, dst, target):
        copy = remote(index, src, dst, target)
        copy.start()
        sent.append(copy)

    def arrive(index, dst):
        remote(index, dst, dst, (t, s)).wait_recv()

    def local(src, dst):
        copy = pltpu.make_async_copy(src, dst, local_sem.at[count["local"]])
        count["local"] += 1
        copy.start()
        return copy

    frames_copy = local(frames, frames_v)
    weights = {
        "q": Weight(wq, wq_v, True),
        "kv": Weight(wkv, wkv_v, False),
        "up": Weight(wup, wup_v, True),
        "od": Folded(od_v, ods_v),
    }
    fold_copies = [local(wlat, wlat_v), local(wo, wo_v), local(wdown, wdown_v)]
    own_copy = {kind: local(weights[kind].src, weights[kind].own()) for kind in ("q", "kv", "up")}
    wconv_copy = local(wconv, wconv_v)

    pl.semaphore_wait(barrier, 17)

    sems = {}

    def far_start(kind):
        w = weights[kind]
        sems[kind, "z"] = take()
        push(sems[kind, "z"], w.src_piece(core, y, x_hi), w.piece(core, y, x), at(dz=4))

    def pair_start(kind):
        w = weights[kind]
        sems[kind, "pair"] = take()
        target = device(core, (x + 3 + 2 * core) % 4, y, z)
        push(sems[kind, "pair"], w.src_half(core), w.pair_half(core), target)

    def pair_share(kind):
        w = weights[kind]
        arrive(sems[kind, "pair"], w.pair_half(core))
        sems[kind, "pair_c"] = take()
        push(sems[kind, "pair_c"], w.pair_half(core), w.pair_half(core), at(dc=1))

    def pair_done(kind):
        arrive(sems[kind, "pair_c"], weights[kind].pair_half(other))

    def row_start(kind):
        w = weights[kind]
        mine = w.piece(core, y, x)
        arrive(sems[kind, "z"], mine)
        for dx in (1, 3, 2):
            sems[kind, "x", dx] = take()
            push(sems[kind, "x", dx], mine, mine, at(dx=dx))

    def column_start(kind):
        w = weights[kind]
        for dx in (1, 3, 2):
            arrive(sems[kind, "x", dx], w.piece(core, y, (x + 4 - dx) % 4))
        mine = w.region(core, y)
        for dy in (1, 3) if kind == "up" else (1, 3, 2):
            sems[kind, "y", dy] = take()
            push(sems[kind, "y", dy], mine, mine, at(dy=dy))
        sems[kind, "c", 0] = take()
        push(sems[kind, "c", 0], mine, mine, at(dc=1))

    def column_relay(kind):
        w = weights[kind]
        for dy, piece in ((1, 0), (3, 1)):
            row = (y + 4 - dy) % 4
            got = w.region(core, row)
            arrive(sems[kind, "y", dy], got)
            half = w.half_region(core, row, piece)
            sems[kind, "y2", dy] = take()
            push(sems[kind, "y2", dy], half, half, at(dy=dy))
            sems[kind, "c", dy] = take()
            push(sems[kind, "c", dy], got, got, at(dc=1))

    def column_share(kind):
        w = weights[kind]
        for dy in (1, 3, 2):
            got = w.region(core, (y + 4 - dy) % 4)
            arrive(sems[kind, "y", dy], got)
            sems[kind, "c", dy] = take()
            push(sems[kind, "c", dy], got, got, at(dc=1))

    def column_end(kind):
        w = weights[kind]
        row = (y + 2) % 4
        for dy, piece in ((1, 0), (3, 1)):
            half = w.half_region(core, row, piece)
            arrive(sems[kind, "y2", dy], half)
            sems[kind, "c2", dy] = take()
            push(sems[kind, "c2", dy], half, half, at(dc=1))

    def far_done(kind):
        w = weights[kind]
        for dy in (0, 1, 3) if kind == "up" else (0, 1, 3, 2):
            arrive(sems[kind, "c", dy], w.region(other, (y + 4 - dy) % 4))
        for dy, piece in ((1, 0), (3, 1)) if kind == "up" else ():
            arrive(sems[kind, "c2", dy], w.half_region(other, (y + 2) % 4, piece))

    for kind in ("q", "kv"):
        far_start(kind)
    for kind in ("q", "kv"):
        pair_start(kind)

    frames_copy.wait()
    row = lax.broadcasted_iota(jnp.int32, (TOKENS, TOKENS), 0)
    col = lax.broadcasted_iota(jnp.int32, (TOKENS, TOKENS), 1)
    turn = (col == (row & 7) * 16 + (row >> 3)).astype(F32).astype(BF16)
    moved = jnp.dot(turn, frames_v[...], preferred_element_type=F32)
    frame_row = lax.broadcasted_iota(jnp.int32, (8, 2048), 0)
    ids = jnp.zeros((8, 2048), jnp.int32)
    for frame in range(8):
        ids = jnp.where(frame_row == frame, actions[frame], ids)
    embedding = jnp.zeros((8, 2048), F32)
    for action in range(8):
        embedding += jnp.where(ids == action, table[action : action + 1, :].astype(F32), 0.0)
    stream = moved.reshape(16, 8, 2048) + embedding[None]
    x_v[0:128, :] = stream.reshape(TOKENS, 2048).astype(BF16)

    token_sems = {}

    def token_send(name, home, away, dz):
        token_sems[name] = take()
        push(token_sems[name], x_v.at[home], x_v.at[away], at(dz=dz))

    token_send("up first", slice(0, 64), slice(128, 192), 1)
    token_send("down last", slice(64, 128), slice(320, 384), 7)

    def token_arrive(name, away):
        arrive(token_sems[name], x_v.at[away])

    def norm_rows(first, last):
        def block(index, carry):
            rows = pl.ds(pl.multiple_of(index * 16, 16), 16)
            n_v[rows, :] = root_scale(x_v[rows, :].astype(F32), norm_gain[...]).astype(BF16)
            return carry

        lax.fori_loop(first // 16, last // 16, block, 0)

    for copy in fold_copies:
        copy.wait()
    od_v[0:128, :] = jnp.dot(wo_v[...], wlat_v[...], preferred_element_type=F32).astype(BF16)
    od_v[128:640, :] = jnp.dot(wdown_v[...], wlat_v[...], preferred_element_type=F32).astype(BF16)
    token_send("up last", slice(64, 128), slice(192, 256), 1)
    token_send("down first", slice(0, 64), slice(256, 320), 7)
    for kind in ("up", "od"):
        far_start(kind)
    for kind in ("q", "kv"):
        row_start(kind)
    ods_v[0] = od_v[...]
    norm_rows(0, 128)
    token_arrive("up first", slice(128, 192))
    token_send("up on", slice(128, 192), slice(384, 448), 1)
    token_arrive("down last", slice(320, 384))
    token_send("down on", slice(320, 384), slice(448, 512), 7)
    for kind in ("q", "kv"):
        column_start(kind)
    for kind in ("q", "kv"):
        pair_share(kind)
    pair_start("up")
    for kind in ("q", "kv"):
        column_share(kind)
    token_arrive("up last", slice(192, 256))
    token_arrive("down first", slice(256, 320))
    row_start("up")
    norm_rows(128, 384)
    pair_start("od")
    row_start("od")
    column_start("up")
    token_arrive("up on", slice(384, 448))
    token_arrive("down on", slice(448, 512))
    norm_rows(384, 512)

    for kind in ("q", "kv"):
        own_copy[kind].wait()
        pair_done(kind)
        far_done(kind)
    routes = (
        (1, slice(0, 128), slice(128, 256)),
        (7, slice(0, 128), slice(256, 384)),
        (2, slice(0, 64), slice(384, 448)),
        (6, slice(64, 128), slice(448, 512)),
    )
    kvt_v[...] = lax.dot_general(
        wkv_v[...], n_v[...], (((1,), (1,)), ((), ())), preferred_element_type=F32
    ).astype(BF16)
    kv_sems = [take() for _ in routes]
    kv_columns = (slice(128, 256), slice(256, 384), slice(384, 512), slice(384, 512))
    for slot, (index, (dz, home, away)) in enumerate(zip(kv_sems, routes)):
        push(index, kvt_v.at[:, kv_columns[slot]], kvr_v.at[slot], at(dz=8 - dz))
    for half in range(2):
        rows = slice(half * 256, half * 256 + 256)
        q_v[rows, :] = jnp.dot(n_v[rows, :], wq_v[...], preferred_element_type=F32).astype(BF16)
    q_sems = [take() for _ in routes]
    q_columns = (slice(512, 1024), slice(1024, 1536), slice(1536, 2048), slice(1536, 2048))
    for slot, (index, (dz, home, away)) in enumerate(zip(q_sems, routes)):
        push(index, q_v.at[away], qr_v.at[home, q_columns[slot]], at(dz=8 - dz))
    qr_v[:, 0:512] = q_v[0:128, :]

    def up_tiles(shard):
        def tile(index, carry):
            columns = pl.ds(pl.multiple_of(shard * 512 + index * 256, 256), 256)
            hidden = jnp.dot(n_v[...], wup_v[:, columns], preferred_element_type=F32)
            h_v[:, columns] = jax.nn.gelu(hidden, approximate=True).astype(BF16)
            return carry

        lax.fori_loop(0, 2, tile, 0)

    column_start("od")
    own_copy["up"].wait()
    up_tiles(0)
    pair_share("up")

    for slot, index in enumerate(kv_sems):
        arrive(index, kvr_v.at[slot])
    later_half = lax.broadcasted_iota(jnp.int32, (8, TOKENS), 1) >= 64
    for index, (plane, block) in enumerate((
        (z, kvt_v[:, 0:128].astype(F32)),
        (z + 1, kvr_v[0].astype(F32)),
        (z + 7, kvr_v[1].astype(F32)),
        (z + 2, kvr_v[2].astype(F32)),
        (z + 6, kvr_v[3].astype(F32)),
    )):
        near_plane, far_plane = plane % 8, (plane + 4) % 8
        places = (
            near_plane * 2 + x_lo,
            near_plane * 2 + 1 - x_lo,
            far_plane * 2,
            far_plane * 2 + 1,
        )
        for shard, place in enumerate(places):
            rows = pl.ds(pl.multiple_of(place * 8, 8), 8)
            for part in range(2):
                found = block[shard * 16 + part * 8 : shard * 16 + part * 8 + 8, :]
                if index == 4:
                    found = jnp.where(later_half, found, kvt_f[part, rows, :])
                kvt_f[part, rows, :] = found
    keys = root_scale(jnp.transpose(kvt_f[0]), qk_gain[1:2, :])
    values = jnp.transpose(kvt_f[1])
    kvg_v[t] = jnp.concatenate([keys, values], axis=1).astype(BF16)
    chip = t // 2
    gather_sem, share_sem = count["sem"], count["sem"] + 7
    count["sem"] += 15

    def gather(step):
        mine = kvg_v.at[t]
        return remote(gather_sem + step - 1, mine, mine, ((t + 2 * step) % 16, s))

    def share(step):
        got = kvg_v.at[(t + 16 - 2 * step) % 16]
        return remote(share_sem + step, got, got, at(dc=1))

    def gather_send(step, carry):
        @pl.when(chip + step < 8)
        def _():
            gather(step).start()

        return carry

    def gather_pass(step, carry):
        @pl.when(chip - step >= 0)
        def _():
            arrive(gather_sem + step - 1, kvg_v.at[(t + 16 - 2 * step) % 16])
            share(step).start()

        return carry

    def gather_wait(step, carry):
        @pl.when(chip - step >= 0)
        def _():
            arrive(share_sem + step, kvg_v.at[(t + 16 - 2 * step + 1 - 2 * core) % 16])

        return carry

    def gather_sent(step, carry):
        @pl.when(chip + step < 8)
        def _():
            gather(step).wait_send()

        @pl.when(chip - step >= 0)
        def _():
            share(step).wait_send()

        return carry

    lax.fori_loop(1, 8, gather_send, 0)

    @pl.when(core == 0)
    def _():
        share(0).start()

    column_relay("up")
    pair_done("up")
    up_tiles(1)
    column_share("od")

    for index, (slot, (dz, home, away)) in zip(q_sems, enumerate(routes)):
        arrive(index, qr_v.at[home, q_columns[slot]])
    for head in range(16):
        query = root_scale(qr_v[:, head * 128 : head * 128 + 128].astype(F32), qk_gain[0:1, :])
        qn_v[:, head] = query.astype(BF16).astype(F32).reshape(16, 8, 128)
    lax.fori_loop(1, 8, gather_pass, 0)

    @pl.when(core == 1)
    def _():
        arrive(share_sem, kvg_v.at[t - 1])

    lax.fori_loop(1, 8, gather_wait, 0)

    def widen(index, carry):
        @pl.when(index <= t)
        def _():
            kvf_v[index] = kvg_v[index].astype(F32).reshape(16, 8, 256)

        @pl.when(index > t)
        def _():
            kvf_v[index] = jnp.zeros((16, 8, 256), F32)

        return carry

    lax.fori_loop(0, 16, widen, 0)
    allowed = col <= t * 8 + (row & 7)
    score_scale = 1.0 / math.sqrt(128)

    def attend(place, carry):
        query = qn_v[place].reshape(128, 128).astype(BF16)
        pair = kvf_v[:, place].reshape(128, 256).astype(BF16)
        scores = lax.dot_general(
            query, pair[:, 0:128], (((1,), (1,)), ((), ())), preferred_element_type=F32
        ) * score_scale
        scores = jnp.where(allowed, scores, MASKED)
        exponent = jnp.exp(scores - jnp.max(scores, axis=-1, keepdims=True))
        exponent = jnp.where(allowed, exponent, 0.0)
        totals = jnp.sum(exponent, axis=-1, keepdims=True)
        mixed = jnp.dot(exponent.astype(BF16), pair[:, 128:256], preferred_element_type=F32)
        mixed = mixed / totals
        rows = pl.ds(pl.multiple_of(place * 8, 8), 8)
        for head in range(16):
            ao_f[rows, head * 128 : head * 128 + 128] = mixed[head * 8 : head * 8 + 8, :]
        return carry

    lax.fori_loop(0, 16, attend, 0, unroll=2)
    ao_v[...] = ao_f[...].astype(BF16)
    at_v[0:128, :] = ao_v[:, 0:512]
    at_sems = [take() for _ in routes]
    for slot, (index, (dz, home, away)) in enumerate(zip(at_sems, routes)):
        push(index, ao_v.at[home, q_columns[slot]], at_v.at[away], at(dz=dz))
    column_end("up")
    pair_share("od")
    far_done("up")
    up_tiles(2)
    up_tiles(3)
    pair_done("od")
    far_done("od")

    for half in (1, 0):
        rows = slice(half * 256, half * 256 + 256)
        ffn = jnp.zeros((256, 512), F32)
        for shard in range(4):
            ffn += jnp.dot(
                h_v[rows, shard * 512 : shard * 512 + 512], ods_v[shard, 128:640, :],
                preferred_element_type=F32,
            )
        ffn_f[rows, :] = ffn
    for index, (dz, home, away) in zip(at_sems, routes):
        arrive(index, at_v.at[away])
    sum_sems = [take() for _ in routes]
    places = ((0, slice(0, 128)), (1, slice(0, 128)), (2, slice(0, 64)), (2, slice(64, 128)))
    for half in (1, 0):
        rows = slice(half * 256, half * 256 + 256)
        part = ffn_f[rows, :]
        for shard in range(4):
            part += jnp.dot(
                at_v[rows, shard * 128 : shard * 128 + 128], ods_v[shard, 0:128, :],
                preferred_element_type=F32,
            )
        p_v[rows, :] = part.astype(BF16)
        for slot in ((2, 3, 1), (0,))[1 - half]:
            dz, home, away = routes[slot]
            lead, span = places[slot]
            push(sum_sems[slot], p_v.at[away], pr_v.at[lead, span], at(dz=8 - dz))
    latent = jnp.dot(x_v[0:128, :], wlat_v[...], preferred_element_type=F32)
    latent += p_v[0:128, :].astype(F32)
    for slot, index in enumerate(sum_sems):
        lead, span = places[slot]
        arrive(index, pr_v.at[lead, span])
    for lead in range(3):
        latent += pr_v[lead].astype(F32)
    lat_v[...] = (latent / (1.0 + jnp.exp(-latent))).astype(BF16)
    halo_sem = take()
    push(halo_sem, lat_v, lb_v, above)

    wconv_copy.wait()
    zero_rows = jnp.zeros((8, 512), F32)

    def right_of(cells):
        wide = cells.astype(F32)
        return jnp.concatenate([wide[8:, :], zero_rows], axis=0).astype(BF16)

    def tap(cells, down, across):
        return jnp.dot(cells, wconv_v[down, across], preferred_element_type=F32)

    o_row = lax.broadcasted_iota(jnp.int32, (256, 256), 0)
    o_col = lax.broadcasted_iota(jnp.int32, (256, 256), 1)
    weave = (o_col == (o_row & 1) * 128 + ((o_row >> 1) & 15) * 8 + (o_row >> 5)).astype(F32)
    weave = weave.astype(BF16)

    def store(parity, even, odd):
        pair = jnp.concatenate([even + bias[...], odd + bias[...]], axis=0).astype(BF16)
        woven = jnp.dot(weave, pair, preferred_element_type=F32).astype(BF16)
        out[:, parity] = woven.reshape(8, 32, 512)

    center = lat_v[...]
    right = right_of(center)
    store(0, tap(center, 1, 1), tap(right, 1, 0) + tap(center, 1, 2))
    odd_even = tap(center, 2, 1)
    odd_odd = tap(right, 2, 0) + tap(center, 2, 2)
    arrive(halo_sem, lb_v)
    under = jnp.where(s < 15, lb_v[...].astype(F32), 0.0).astype(BF16)
    corner = right_of(under)
    store(1, odd_even + tap(under, 0, 1), odd_odd + tap(corner, 0, 0) + tap(under, 0, 2))

    for copy in sent:
        copy.wait_send()

    @pl.when(core == 0)
    def _():
        share(0).wait_send()

    lax.fori_loop(1, 8, gather_sent, 0)


def per_device(
    frames, actions, action_table, norm_gain, w_q, w_kv, qk_gain, w_o, w_up, w_down, w_lat, w_conv,
    conv_bias,
):
    w_kv = jnp.transpose(w_kv, (1, 2, 0)).reshape(16, 2048)
    vmem, anywhere = pl.BlockSpec(memory_space=pltpu.VMEM), pl.BlockSpec(memory_space=pl.ANY)
    smem = pl.BlockSpec(memory_space=pltpu.SMEM)
    flops = 2 * 512 * 2048 * (512 * 2 + 64 + 2048 + 512) + 2 * 128 * 512 * (2048 + 9 * 512)
    return pl.pallas_call(
        kernel,
        out_shape=jax.ShapeDtypeStruct((8, 2, 32, 512), BF16),
        in_specs=[
            anywhere, smem, vmem, vmem, anywhere, anywhere, vmem, anywhere, anywhere, anywhere,
            anywhere, anywhere, vmem,
        ],
        out_specs=vmem,
        scratch_shapes=[
            pltpu.VMEM((128, 2048), BF16),
            pltpu.VMEM((2048, 512), BF16),
            pltpu.VMEM((64, 2048), BF16),
            pltpu.VMEM((2048, 2048), BF16),
            pltpu.VMEM((128, 2048), BF16),
            pltpu.VMEM((512, 2048), BF16),
            pltpu.VMEM((2048, 512), BF16),
            pltpu.VMEM((3, 3, 512, 512), BF16),
            pltpu.VMEM((640, 512), BF16),
            pltpu.VMEM((4, 640, 512), BF16),
            pltpu.VMEM((512, 2048), BF16),
            pltpu.VMEM((512, 2048), BF16),
            pltpu.VMEM((512, 512), BF16),
            pltpu.VMEM((128, 2048), BF16),
            pltpu.VMEM((64, 512), BF16),
            pltpu.VMEM((4, 64, 128), BF16),
            pltpu.VMEM((2, 128, 128), F32),
            pltpu.VMEM((16, 128, 256), BF16),
            pltpu.VMEM((16, 16, 8, 256), F32),
            pltpu.VMEM((16, 16, 8, 128), F32),
            pltpu.VMEM((128, 2048), F32),
            pltpu.VMEM((128, 2048), BF16),
            pltpu.VMEM((512, 512), BF16),
            pltpu.VMEM((512, 2048), BF16),
            pltpu.VMEM((512, 512), BF16),
            pltpu.VMEM((3, 128, 512), BF16),
            pltpu.VMEM((512, 512), F32),
            pltpu.VMEM((128, 512), BF16),
            pltpu.VMEM((128, 512), BF16),
            pltpu.SemaphoreType.DMA((N_SEMS,)),
            pltpu.SemaphoreType.DMA((N_SEMS,)),
            pltpu.SemaphoreType.DMA((8,)),
        ],
        compiler_params=pltpu.CompilerParams(
            collective_id=1, has_side_effects=True, vmem_limit_bytes=60 * 1024 * 1024
        ),
        cost_estimate=pl.CostEstimate(flops=flops, bytes_accessed=14000000, transcendentals=0),
        name="block",
    )(
        frames.reshape(128, 2048),
        actions,
        action_table,
        norm_gain.reshape(1, 2048),
        w_q,
        w_kv,
        qk_gain,
        w_o,
        w_up,
        w_down,
        w_lat,
        w_conv,
        conv_bias.reshape(1, 512),
    )


def solution(mesh):
    return jax.shard_map(
        per_device,
        mesh=mesh,
        in_specs=(
            P("tm", "space", None, None),
            P("tm"),
            P(),
            P(),
            P(None, "space"),
            P(None, None, "space"),
            P(),
            P("space", None),
            P(None, "space"),
            P("space", None),
            P(),
            P(),
            P(),
        ),
        out_specs=P("tm", "space", None, None),
        check_vma=False,
    )
```

```python
import functools
import math

import jax
import jax.numpy as jnp
from jax import lax
from jax.experimental import pallas as pl
from jax.experimental.pallas import tpu as pltpu
from jax.sharding import PartitionSpec as P

MESH = pl.DeviceIdType.MESH
EPS = 1e-06
MASKED = -1e30
F32 = jnp.float32
BF16 = jnp.bfloat16
UPS = ("up0", "up1")
N_SEMS = 128
TOKENS = 128


def device(core, x, y, z):
    return ((y * 2 + x // 2) * 2 + core, z * 2 + x % 2)


class Weight:
    def __init__(self, src, dst, along_rows):
        self.src, self.dst, self.along_rows = src, dst, along_rows
        self.size = src.shape[1] if along_rows else src.shape[0]

    def cut(self, ref, start, length, shard=None, shards=1):
        start = pl.multiple_of(start, 128)
        if shard is None:
            across = slice(None)
        elif isinstance(shard, int):
            across = slice(shard * self.size, (shard + shards) * self.size)
        else:
            step = 128 if self.along_rows else 16
            across = pl.ds(pl.multiple_of(shard * self.size, step), shards * self.size)
        if self.along_rows:
            return ref.at[pl.ds(start, length), across]
        return ref.at[across, pl.ds(start, length)]

    def own(self):
        return self.cut(self.dst, 0, 2048, 0)

    def src_half(self, core):
        return self.cut(self.src, core * 1024, 1024)

    def pair_half(self, core):
        return self.cut(self.dst, core * 1024, 1024, 1)

    def src_piece(self, core, y, x_hi):
        return self.cut(self.src, (core * 8 + y * 2 + x_hi) * 128, 128)

    def piece(self, core, y, x):
        return self.cut(self.dst, (core * 8 + y * 2 + x // 2) * 128, 128, 2 + x % 2)

    def region(self, core, y):
        return self.cut(self.dst, (core * 8 + y * 2) * 128, 256, 2, 2)

    def half_region(self, core, y, x_hi):
        return self.cut(self.dst, (core * 8 + y * 2 + x_hi) * 128, 128, 2, 2)


class Folded(Weight):
    def __init__(self, src, dst):
        self.src, self.dst = src, dst

    def own(self):
        return self.dst.at[0]

    def src_half(self, core):
        return self.src.at[pl.ds(pl.multiple_of(core * 320, 320), 320)]

    def pair_half(self, core):
        return self.dst.at[1, pl.ds(pl.multiple_of(core * 320, 320), 320)]

    def block(self, core, y):
        rows = pl.ds(pl.multiple_of((core * 2 + y // 2) * 160, 160), 160)
        return rows, (y % 2) * 256

    def src_piece(self, core, y, x_hi):
        rows, column = self.block(core, y)
        return self.src.at[rows, pl.ds(pl.multiple_of(column + x_hi * 128, 128), 128)]

    def piece(self, core, y, x):
        rows, column = self.block(core, y)
        columns = pl.ds(pl.multiple_of(column + x // 2 * 128, 128), 128)
        return self.dst.at[2 + x % 2, rows, columns]

    def region(self, core, y):
        rows, column = self.block(core, y)
        return self.dst.at[2:4, rows, pl.ds(pl.multiple_of(column, 256), 256)]

    def half_region(self, core, y, x_hi):
        rows, column = self.block(core, y)
        return self.dst.at[2:4, rows, pl.ds(pl.multiple_of(column + x_hi * 128, 128), 128)]


def root_scale(values, gain):
    return values * lax.rsqrt(jnp.mean(values * values, axis=-1, keepdims=True) + EPS) * gain


def kernel(
    frames, actions, table, norm_gain, wq, wkv, qk_gain, wo, wup, wdown, wlat, wconv, bias,
    out,
    frames_v, wq_v, wkv_v, wup_v, wo_v, wdown_v, wlat_v, wconv_v, od_v, ods_v,
    x_v, n_v, q_v, qr_v, kvt_v, kvr_v, kvt_f, kvg_v, kvf_v, qn_v, ao_f, ao_v, at_v, h_v, p_v, pr_v, ffn_f,
    lat_v, lb_v, send_sem, recv_sem, local_sem,
):
    t, s = lax.axis_index("tm"), lax.axis_index("space")
    core, x_hi, y = t % 2, (t // 2) % 2, t // 4
    x_lo, z = s % 2, s // 2
    x = x_hi * 2 + x_lo
    other = 1 - core

    def at(dc=0, dx=0, dy=0, dz=0):
        return device((core + dc) % 2, (x + dx) % 4, (y + dy) % 4, (z + dz) % 8)

    above, below = (t, (s + 15) % 16), (t, (s + 1) % 16)
    barrier = pltpu.get_barrier_semaphore()
    near = [at(dz=1), at(dz=7), at(dz=2), at(dz=6), at(dz=4), at(dx=1), at(dx=3)]
    for partner in near + [above, below, at(dc=1)]:
        pl.semaphore_signal(barrier, inc=1, device_id=partner, device_id_type=MESH)

    def greet(step, carry):
        pl.semaphore_signal(
            barrier, inc=1, device_id=((t + 2 * step) % 16, s), device_id_type=MESH
        )
        return carry

    lax.fori_loop(1, 8, greet, 0)

    count = {"sem": 0, "local": 0}
    sent = []

    def take():
        count["sem"] += 1
        return count["sem"] - 1

    def remote(index, src, dst, target):
        return pltpu.make_async_remote_copy(
            src_ref=src, dst_ref=dst, send_sem=send_sem.at[index], recv_sem=recv_sem.at[index],
            device_id=target, device_id_type=MESH,
        )

    def push(index, src, dst, target):
        copy = remote(index, src, dst, target)
        copy.start()
        sent.append(copy)

    def arrive(index, dst):
        remote(index, dst, dst, (t, s)).wait_recv()

    def local(src, dst):
        copy = pltpu.make_async_copy(src, dst, local_sem.at[count["local"]])
        count["local"] += 1
        copy.start()
        return copy

    frames_copy = local(frames, frames_v)
    weights = {
        "q": Weight(wq, wq_v, True),
        "kv": Weight(wkv, wkv_v, False),
        "up0": Weight(wup.at[:, 0:256], wup_v.at[0], True),
        "up1": Weight(wup.at[:, 256:512], wup_v.at[1], True),
        "od": Folded(od_v, ods_v),
    }
    fold_copies = [local(wlat, wlat_v), local(wo, wo_v), local(wdown, wdown_v)]
    own_copy = {kind: local(weights[kind].src, weights[kind].own()) for kind in ("q", "kv") + UPS}
    wconv_copy = local(wconv, wconv_v)

    pl.semaphore_wait(barrier, 17)

    sems = {}

    def far_start(kind):
        w = weights[kind]
        sems[kind, "z"] = take()
        push(sems[kind, "z"], w.src_piece(core, y, x_hi), w.piece(core, y, x), at(dz=4))

    def pair_start(kind):
        w = weights[kind]
        sems[kind, "pair"] = take()
        target = device(core, (x + 3 + 2 * core) % 4, y, z)
        push(sems[kind, "pair"], w.src_half(core), w.pair_half(core), target)

    def pair_share(kind):
        w = weights[kind]
        arrive(sems[kind, "pair"], w.pair_half(core))
        sems[kind, "pair_c"] = take()
        push(sems[kind, "pair_c"], w.pair_half(core), w.pair_half(core), at(dc=1))

    def pair_done(kind):
        arrive(sems[kind, "pair_c"], weights[kind].pair_half(other))

    def row_start(kind):
        w = weights[kind]
        mine = w.piece(core, y, x)
        arrive(sems[kind, "z"], mine)
        for dx in (1, 3, 2):
            sems[kind, "x", dx] = take()
            push(sems[kind, "x", dx], mine, mine, at(dx=dx))

    def column_start(kind):
        w = weights[kind]
        for dx in (1, 3, 2):
            arrive(sems[kind, "x", dx], w.piece(core, y, (x + 4 - dx) % 4))
        mine = w.region(core, y)
        for dy in (1, 3) if kind in UPS else (1, 3, 2):
            sems[kind, "y", dy] = take()
            push(sems[kind, "y", dy], mine, mine, at(dy=dy))
        sems[kind, "c", 0] = take()
        push(sems[kind, "c", 0], mine, mine, at(dc=1))

    def column_relay(kind):
        w = weights[kind]
        for dy, piece in ((1, 0), (3, 1)):
            row = (y + 4 - dy) % 4
            got = w.region(core, row)
            arrive(sems[kind, "y", dy], got)
            half = w.half_region(core, row, piece)
            sems[kind, "y2", dy] = take()
            push(sems[kind, "y2", dy], half, half, at(dy=dy))
            sems[kind, "c", dy] = take()
            push(sems[kind, "c", dy], got, got, at(dc=1))

    def column_share(kind):
        w = weights[kind]
        for dy in (1, 3, 2):
            got = w.region(core, (y + 4 - dy) % 4)
            arrive(sems[kind, "y", dy], got)
            sems[kind, "c", dy] = take()
            push(sems[kind, "c", dy], got, got, at(dc=1))

    def column_end(kind):
        w = weights[kind]
        row = (y + 2) % 4
        for dy, piece in ((1, 0), (3, 1)):
            half = w.half_region(core, row, piece)
            arrive(sems[kind, "y2", dy], half)
            sems[kind, "c2", dy] = take()
            push(sems[kind, "c2", dy], half, half, at(dc=1))

    def far_done(kind):
        w = weights[kind]
        for dy in (0, 1, 3) if kind in UPS else (0, 1, 3, 2):
            arrive(sems[kind, "c", dy], w.region(other, (y + 4 - dy) % 4))
        for dy, piece in ((1, 0), (3, 1)) if kind in UPS else ():
            arrive(sems[kind, "c2", dy], w.half_region(other, (y + 2) % 4, piece))

    for kind in ("q", "kv") + UPS:
        far_start(kind)
    for kind in ("q", "kv"):
        pair_start(kind)

    frames_copy.wait()
    row = lax.broadcasted_iota(jnp.int32, (TOKENS, TOKENS), 0)
    col = lax.broadcasted_iota(jnp.int32, (TOKENS, TOKENS), 1)
    turn = (col == (row & 7) * 16 + (row >> 3)).astype(F32).astype(BF16)
    moved = jnp.dot(turn, frames_v[...], preferred_element_type=F32)
    frame_row = lax.broadcasted_iota(jnp.int32, (8, 2048), 0)
    ids = jnp.zeros((8, 2048), jnp.int32)
    for frame in range(8):
        ids = jnp.where(frame_row == frame, actions[frame], ids)
    embedding = jnp.zeros((8, 2048), F32)
    for action in range(8):
        embedding += jnp.where(ids == action, table[action : action + 1, :].astype(F32), 0.0)
    stream = moved.reshape(16, 8, 2048) + embedding[None]
    x_v[0:128, :] = stream.reshape(TOKENS, 2048).astype(BF16)

    token_sems = {}

    def token_send(name, home, away, dz):
        token_sems[name] = take()
        push(token_sems[name], x_v.at[home], x_v.at[away], at(dz=dz))

    token_send("up first", slice(0, 64), slice(128, 192), 1)
    token_send("down last", slice(64, 128), slice(320, 384), 7)

    def token_arrive(name, away):
        arrive(token_sems[name], x_v.at[away])

    def norm_rows(first, last):
        def block(index, carry):
            rows = pl.ds(pl.multiple_of(index * 16, 16), 16)
            n_v[rows, :] = root_scale(x_v[rows, :].astype(F32), norm_gain[...]).astype(BF16)
            return carry

        lax.fori_loop(first // 16, last // 16, block, 0)

    for copy in fold_copies:
        copy.wait()
    od_v[0:128, :] = jnp.dot(wo_v[...], wlat_v[...], preferred_element_type=F32).astype(BF16)
    od_v[128:640, :] = jnp.dot(wdown_v[...], wlat_v[...], preferred_element_type=F32).astype(BF16)
    token_send("up last", slice(64, 128), slice(192, 256), 1)
    token_send("down first", slice(0, 64), slice(256, 320), 7)
    far_start("od")
    for kind in ("q", "kv"):
        row_start(kind)
    ods_v[0] = od_v[...]
    norm_rows(0, 128)
    token_arrive("up first", slice(128, 192))
    token_send("up on", slice(128, 192), slice(384, 448), 1)
    token_arrive("down last", slice(320, 384))
    token_send("down on", slice(320, 384), slice(448, 512), 7)
    for kind in ("q", "kv"):
        column_start(kind)
    for kind in UPS:
        row_start(kind)
    for kind in ("q", "kv"):
        pair_share(kind)
    for kind in ("q", "kv"):
        column_share(kind)
    for kind in UPS:
        column_start(kind)
    for kind in UPS:
        pair_start(kind)
    token_arrive("up last", slice(192, 256))
    token_arrive("down first", slice(256, 320))
    norm_rows(128, 384)
    row_start("od")
    pair_start("od")
    column_relay("up0")
    token_arrive("up on", slice(384, 448))
    token_arrive("down on", slice(448, 512))
    norm_rows(384, 512)

    column_relay("up1")
    for kind in ("q", "kv"):
        own_copy[kind].wait()
        pair_done(kind)
        far_done(kind)
    routes = (
        (1, slice(0, 128), slice(128, 256)),
        (7, slice(0, 128), slice(256, 384)),
        (2, slice(0, 64), slice(384, 448)),
        (6, slice(64, 128), slice(448, 512)),
    )
    kvt_v[...] = lax.dot_general(
        wkv_v[...], n_v[...], (((1,), (1,)), ((), ())), preferred_element_type=F32
    ).astype(BF16)
    kv_sems = [take() for _ in routes]
    kv_columns = (slice(128, 256), slice(256, 384), slice(384, 512), slice(384, 512))
    for slot, (index, (dz, home, away)) in enumerate(zip(kv_sems, routes)):
        push(index, kvt_v.at[:, kv_columns[slot]], kvr_v.at[slot], at(dz=8 - dz))
    q_sems = [take() for _ in routes]
    q_columns = (slice(512, 1024), slice(1024, 1536), slice(1536, 2048), slice(1536, 2048))
    for half, slots in ((1, (2, 3, 1)), (0, (0,))):
        rows = slice(half * 256, half * 256 + 256)
        q_v[rows, :] = jnp.dot(n_v[rows, :], wq_v[...], preferred_element_type=F32).astype(BF16)
        for slot in slots:
            dz, home, away = routes[slot]
            push(q_sems[slot], q_v.at[away], qr_v.at[home, q_columns[slot]], at(dz=8 - dz))
    qr_v[:, 0:512] = q_v[0:128, :]

    def up_tile(chunk, shard):
        place = chunk * 1024 + shard * 256
        weight = wup_v[chunk, :, shard * 256 : shard * 256 + 256]
        for half in range(2):
            rows = slice(half * 256, half * 256 + 256)
            hidden = jnp.dot(n_v[rows, :], weight, preferred_element_type=F32)
            h_v[rows, place : place + 256] = jax.nn.gelu(hidden, approximate=True).astype(BF16)

    column_start("od")
    for chunk, kind in enumerate(UPS):
        own_copy[kind].wait()
        up_tile(chunk, 0)
    for kind in UPS:
        pair_share(kind)

    for slot, index in enumerate(kv_sems):
        arrive(index, kvr_v.at[slot])
    later_half = lax.broadcasted_iota(jnp.int32, (8, TOKENS), 1) >= 64
    for index, (plane, block) in enumerate((
        (z, kvt_v[:, 0:128].astype(F32)),
        (z + 1, kvr_v[0].astype(F32)),
        (z + 7, kvr_v[1].astype(F32)),
        (z + 2, kvr_v[2].astype(F32)),
        (z + 6, kvr_v[3].astype(F32)),
    )):
        near_plane, far_plane = plane % 8, (plane + 4) % 8
        places = (
            near_plane * 2 + x_lo,
            near_plane * 2 + 1 - x_lo,
            far_plane * 2,
            far_plane * 2 + 1,
        )
        for shard, place in enumerate(places):
            rows = pl.ds(pl.multiple_of(place * 8, 8), 8)
            for part in range(2):
                found = block[shard * 16 + part * 8 : shard * 16 + part * 8 + 8, :]
                if index == 4:
                    found = jnp.where(later_half, found, kvt_f[part, rows, :])
                kvt_f[part, rows, :] = found
    keys = root_scale(jnp.transpose(kvt_f[0]), qk_gain[1:2, :])
    values = jnp.transpose(kvt_f[1])
    kvg_v[t] = jnp.concatenate([keys, values], axis=1).astype(BF16)
    chip = t // 2
    gather_sem, share_sem = count["sem"], count["sem"] + 7
    count["sem"] += 15

    def gather(step):
        mine = kvg_v.at[t]
        return remote(gather_sem + step - 1, mine, mine, ((t + 2 * step) % 16, s))

    def share(step):
        got = kvg_v.at[(t + 16 - 2 * step) % 16]
        return remote(share_sem + step, got, got, at(dc=1))

    def gather_send(step, carry):
        @pl.when(chip + step < 8)
        def _():
            gather(step).start()

        return carry

    def gather_pass(step, carry):
        @pl.when(chip - step >= 0)
        def _():
            arrive(gather_sem + step - 1, kvg_v.at[(t + 16 - 2 * step) % 16])
            share(step).start()

        return carry

    def gather_wait(step, carry):
        @pl.when(chip - step >= 0)
        def _():
            arrive(share_sem + step, kvg_v.at[(t + 16 - 2 * step + 1 - 2 * core) % 16])

        return carry

    def gather_sent(step, carry):
        @pl.when(chip + step < 8)
        def _():
            gather(step).wait_send()

        @pl.when(chip - step >= 0)
        def _():
            share(step).wait_send()

        return carry

    lax.fori_loop(1, 8, gather_send, 0)

    @pl.when(core == 0)
    def _():
        share(0).start()

    for chunk, kind in enumerate(UPS):
        pair_done(kind)
        up_tile(chunk, 1)
    column_share("od")
    column_end("up0")

    for index, (slot, (dz, home, away)) in zip(q_sems, enumerate(routes)):
        arrive(index, qr_v.at[home, q_columns[slot]])
    for head in range(16):
        query = root_scale(qr_v[:, head * 128 : head * 128 + 128].astype(F32), qk_gain[0:1, :])
        qn_v[:, head] = query.astype(BF16).astype(F32).reshape(16, 8, 128)
    lax.fori_loop(1, 8, gather_pass, 0)

    @pl.when(core == 1)
    def _():
        arrive(share_sem, kvg_v.at[t - 1])

    lax.fori_loop(1, 8, gather_wait, 0)

    def widen(index, carry):
        @pl.when(index <= t)
        def _():
            kvf_v[index] = kvg_v[index].astype(F32).reshape(16, 8, 256)

        @pl.when(index > t)
        def _():
            kvf_v[index] = jnp.zeros((16, 8, 256), F32)

        return carry

    lax.fori_loop(0, 16, widen, 0)
    allowed = col <= t * 8 + (row & 7)
    score_scale = 1.0 / math.sqrt(128)

    def attend(place, carry):
        query = qn_v[place].reshape(128, 128).astype(BF16)
        pair = kvf_v[:, place].reshape(128, 256).astype(BF16)
        scores = lax.dot_general(
            query, pair[:, 0:128], (((1,), (1,)), ((), ())), preferred_element_type=F32
        ) * score_scale
        scores = jnp.where(allowed, scores, MASKED)
        exponent = jnp.exp(scores - jnp.max(scores, axis=-1, keepdims=True))
        exponent = jnp.where(allowed, exponent, 0.0)
        totals = jnp.sum(exponent, axis=-1, keepdims=True)
        mixed = jnp.dot(exponent.astype(BF16), pair[:, 128:256], preferred_element_type=F32)
        mixed = mixed / totals
        rows = pl.ds(pl.multiple_of(place * 8, 8), 8)
        for head in range(16):
            ao_f[rows, head * 128 : head * 128 + 128] = mixed[head * 8 : head * 8 + 8, :]
        return carry

    at_sems = []
    sends = (
        ((1, 0, slice(128, 192)), (7, 1, slice(256, 320)), (2, 2, slice(384, 448))),
        ((1, 0, slice(192, 256)), (7, 1, slice(320, 384)), (6, 2, slice(448, 512))),
    )
    for half in range(2):
        lax.fori_loop(half * 8, half * 8 + 8, attend, 0, unroll=4)
        home = slice(half * 64, half * 64 + 64)
        ao_v[home, :] = ao_f[home, :].astype(BF16)
        for dz, slot, away in sends[half]:
            at_sems.append((take(), away))
            push(at_sems[-1][0], ao_v.at[home, q_columns[slot]], at_v.at[away], at(dz=dz))
    at_v[0:128, :] = ao_v[:, 0:512]

    column_end("up1")
    pair_share("od")
    for chunk, kind in enumerate(UPS):
        far_done(kind)
        up_tile(chunk, 2)
        up_tile(chunk, 3)
    pair_done("od")
    far_done("od")

    for half in (1, 0):
        rows = slice(half * 256, half * 256 + 256)
        ffn = jnp.zeros((256, 512), F32)
        for place in range(8):
            chunk, shard = place // 4, place % 4
            ffn += jnp.dot(
                h_v[rows, place * 256 : place * 256 + 256],
                ods_v[shard, 128 + chunk * 256 : 384 + chunk * 256, :],
                preferred_element_type=F32,
            )
        ffn_f[rows, :] = ffn
    for index, away in at_sems:
        arrive(index, at_v.at[away])
    sum_sems = [take() for _ in routes]
    places = ((0, slice(0, 128)), (1, slice(0, 128)), (2, slice(0, 64)), (2, slice(64, 128)))
    for half in (1, 0):
        rows = slice(half * 256, half * 256 + 256)
        part = ffn_f[rows, :]
        for shard in range(4):
            part += jnp.dot(
                at_v[rows, shard * 128 : shard * 128 + 128], ods_v[shard, 0:128, :],
                preferred_element_type=F32,
            )
        p_v[rows, :] = part.astype(BF16)
        for slot in ((2, 3, 1), (0,))[1 - half]:
            dz, home, away = routes[slot]
            lead, span = places[slot]
            push(sum_sems[slot], p_v.at[away], pr_v.at[lead, span], at(dz=8 - dz))
    latent = jnp.dot(x_v[0:128, :], wlat_v[...], preferred_element_type=F32)
    latent += p_v[0:128, :].astype(F32)
    for slot, index in enumerate(sum_sems):
        lead, span = places[slot]
        arrive(index, pr_v.at[lead, span])
    for lead in range(3):
        latent += pr_v[lead].astype(F32)
    lat_v[...] = (latent / (1.0 + jnp.exp(-latent))).astype(BF16)
    halo_sem = take()
    push(halo_sem, lat_v, lb_v, above)

    wconv_copy.wait()
    zero_rows = jnp.zeros((8, 512), F32)

    def right_of(cells):
        wide = cells.astype(F32)
        return jnp.concatenate([wide[8:, :], zero_rows], axis=0).astype(BF16)

    def tap(cells, down, across):
        return jnp.dot(cells, wconv_v[down, across], preferred_element_type=F32)

    o_row = lax.broadcasted_iota(jnp.int32, (256, 256), 0)
    o_col = lax.broadcasted_iota(jnp.int32, (256, 256), 1)
    weave = (o_col == (o_row & 1) * 128 + ((o_row >> 1) & 15) * 8 + (o_row >> 5)).astype(F32)
    weave = weave.astype(BF16)

    def store(parity, even, odd):
        pair = jnp.concatenate([even + bias[...], odd + bias[...]], axis=0).astype(BF16)
        woven = jnp.dot(weave, pair, preferred_element_type=F32).astype(BF16)
        out[:, parity] = woven.reshape(8, 32, 512)

    center = lat_v[...]
    right = right_of(center)
    store(0, tap(center, 1, 1), tap(right, 1, 0) + tap(center, 1, 2))
    odd_even = tap(center, 2, 1)
    odd_odd = tap(right, 2, 0) + tap(center, 2, 2)
    arrive(halo_sem, lb_v)
    under = jnp.where(s < 15, lb_v[...].astype(F32), 0.0).astype(BF16)
    corner = right_of(under)
    store(1, odd_even + tap(under, 0, 1), odd_odd + tap(corner, 0, 0) + tap(under, 0, 2))

    for copy in sent:
        copy.wait_send()

    @pl.when(core == 0)
    def _():
        share(0).wait_send()

    lax.fori_loop(1, 8, gather_sent, 0)


def per_device(
    frames, actions, action_table, norm_gain, w_q, w_kv, qk_gain, w_o, w_up, w_down, w_lat, w_conv,
    conv_bias,
):
    w_kv = jnp.transpose(w_kv, (1, 2, 0)).reshape(16, 2048)
    vmem, anywhere = pl.BlockSpec(memory_space=pltpu.VMEM), pl.BlockSpec(memory_space=pl.ANY)
    smem = pl.BlockSpec(memory_space=pltpu.SMEM)
    flops = 2 * 512 * 2048 * (512 * 2 + 64 + 2048 + 512) + 2 * 128 * 512 * (2048 + 9 * 512)
    return pl.pallas_call(
        kernel,
        out_shape=jax.ShapeDtypeStruct((8, 2, 32, 512), BF16),
        in_specs=[
            anywhere, smem, vmem, vmem, anywhere, anywhere, vmem, anywhere, anywhere, anywhere,
            anywhere, anywhere, vmem,
        ],
        out_specs=vmem,
        scratch_shapes=[
            pltpu.VMEM((128, 2048), BF16),
            pltpu.VMEM((2048, 512), BF16),
            pltpu.VMEM((64, 2048), BF16),
            pltpu.VMEM((2, 2048, 1024), BF16),
            pltpu.VMEM((128, 2048), BF16),
            pltpu.VMEM((512, 2048), BF16),
            pltpu.VMEM((2048, 512), BF16),
            pltpu.VMEM((3, 3, 512, 512), BF16),
            pltpu.VMEM((640, 512), BF16),
            pltpu.VMEM((4, 640, 512), BF16),
            pltpu.VMEM((512, 2048), BF16),
            pltpu.VMEM((512, 2048), BF16),
            pltpu.VMEM((512, 512), BF16),
            pltpu.VMEM((128, 2048), BF16),
            pltpu.VMEM((64, 512), BF16),
            pltpu.VMEM((4, 64, 128), BF16),
            pltpu.VMEM((2, 128, 128), F32),
            pltpu.VMEM((16, 128, 256), BF16),
            pltpu.VMEM((16, 16, 8, 256), F32),
            pltpu.VMEM((16, 16, 8, 128), F32),
            pltpu.VMEM((128, 2048), F32),
            pltpu.VMEM((128, 2048), BF16),
            pltpu.VMEM((512, 512), BF16),
            pltpu.VMEM((512, 2048), BF16),
            pltpu.VMEM((512, 512), BF16),
            pltpu.VMEM((3, 128, 512), BF16),
            pltpu.VMEM((512, 512), F32),
            pltpu.VMEM((128, 512), BF16),
            pltpu.VMEM((128, 512), BF16),
            pltpu.SemaphoreType.DMA((N_SEMS,)),
            pltpu.SemaphoreType.DMA((N_SEMS,)),
            pltpu.SemaphoreType.DMA((9,)),
        ],
        compiler_params=pltpu.CompilerParams(
            collective_id=1, has_side_effects=True, vmem_limit_bytes=60 * 1024 * 1024
        ),
        cost_estimate=pl.CostEstimate(flops=flops, bytes_accessed=14000000, transcendentals=0),
        name="block",
    )(
        frames.reshape(128, 2048),
        actions,
        action_table,
        norm_gain.reshape(1, 2048),
        w_q,
        w_kv,
        qk_gain,
        w_o,
        w_up,
        w_down,
        w_lat,
        w_conv,
        conv_bias.reshape(1, 512),
    )


def solution(mesh):
    return jax.shard_map(
        per_device,
        mesh=mesh,
        in_specs=(
            P("tm", "space", None, None),
            P("tm"),
            P(),
            P(),
            P(None, "space"),
            P(None, None, "space"),
            P(),
            P("space", None),
            P(None, "space"),
            P("space", None),
            P(),
            P(),
            P(),
        ),
        out_specs=P("tm", "space", None, None),
        check_vma=False,
    )
```

```python
import functools
import math

import jax
import jax.numpy as jnp
from jax import lax
from jax.experimental import pallas as pl
from jax.experimental.pallas import tpu as pltpu
from jax.sharding import PartitionSpec as P

MESH = pl.DeviceIdType.MESH
EPS = 1e-06
MASKED = -1e30
F32 = jnp.float32
BF16 = jnp.bfloat16
UPS = ("up0", "up1")
N_SEMS = 128
TOKENS = 128


def device(core, x, y, z):
    return ((y * 2 + x // 2) * 2 + core, z * 2 + x % 2)


class Weight:
    def __init__(self, src, dst, along_rows):
        self.src, self.dst, self.along_rows = src, dst, along_rows
        self.size = src.shape[1] if along_rows else src.shape[0]

    def cut(self, ref, start, length, shard=None, shards=1):
        start = pl.multiple_of(start, 128)
        if shard is None:
            across = slice(None)
        elif isinstance(shard, int):
            across = slice(shard * self.size, (shard + shards) * self.size)
        else:
            step = 128 if self.along_rows else 16
            across = pl.ds(pl.multiple_of(shard * self.size, step), shards * self.size)
        if self.along_rows:
            return ref.at[pl.ds(start, length), across]
        return ref.at[across, pl.ds(start, length)]

    def own(self):
        return self.cut(self.dst, 0, 2048, 0)

    def src_half(self, core):
        return self.cut(self.src, core * 1024, 1024)

    def pair_half(self, core):
        return self.cut(self.dst, core * 1024, 1024, 1)

    def src_piece(self, core, y, x_hi):
        return self.cut(self.src, (core * 8 + y * 2 + x_hi) * 128, 128)

    def piece(self, core, y, x):
        return self.cut(self.dst, (core * 8 + y * 2 + x // 2) * 128, 128, 2 + x % 2)

    def region(self, core, y):
        return self.cut(self.dst, (core * 8 + y * 2) * 128, 256, 2, 2)

    def half_region(self, core, y, x_hi):
        return self.cut(self.dst, (core * 8 + y * 2 + x_hi) * 128, 128, 2, 2)


class Folded(Weight):
    def __init__(self, src, dst):
        self.src, self.dst = src, dst

    def own(self):
        return self.dst.at[0]

    def src_half(self, core):
        return self.src.at[pl.ds(pl.multiple_of(core * 320, 320), 320)]

    def pair_half(self, core):
        return self.dst.at[1, pl.ds(pl.multiple_of(core * 320, 320), 320)]

    def block(self, core, y):
        rows = pl.ds(pl.multiple_of((core * 2 + y // 2) * 160, 160), 160)
        return rows, (y % 2) * 256

    def src_piece(self, core, y, x_hi):
        rows, column = self.block(core, y)
        return self.src.at[rows, pl.ds(pl.multiple_of(column + x_hi * 128, 128), 128)]

    def piece(self, core, y, x):
        rows, column = self.block(core, y)
        columns = pl.ds(pl.multiple_of(column + x // 2 * 128, 128), 128)
        return self.dst.at[2 + x % 2, rows, columns]

    def region(self, core, y):
        rows, column = self.block(core, y)
        return self.dst.at[2:4, rows, pl.ds(pl.multiple_of(column, 256), 256)]

    def half_region(self, core, y, x_hi):
        rows, column = self.block(core, y)
        return self.dst.at[2:4, rows, pl.ds(pl.multiple_of(column + x_hi * 128, 128), 128)]


def root_scale(values, gain):
    return values * lax.rsqrt(jnp.mean(values * values, axis=-1, keepdims=True) + EPS) * gain


def kernel(
    frames, actions, table, norm_gain, wq, wkv, qk_gain, wo, wup, wdown, wlat, wconv, bias,
    out,
    frames_v, wq_v, wkv_v, wup_v, wo_v, wdown_v, wlat_v, wconv_v, od_v, ods_v,
    x_v, n_v, q_v, qr_v, kvt_v, kvr_v, kvt_f, kvg_v, kvf_v, qn_v, ao_f, ao_v, at_v, h_v, p_v, pr_v, ffn_f,
    lat_v, lb_v, send_sem, recv_sem, local_sem,
):
    t, s = lax.axis_index("tm"), lax.axis_index("space")
    core, x_hi, y = t % 2, (t // 2) % 2, t // 4
    x_lo, z = s % 2, s // 2
    x = x_hi * 2 + x_lo
    other = 1 - core

    def at(dc=0, dx=0, dy=0, dz=0):
        return device((core + dc) % 2, (x + dx) % 4, (y + dy) % 4, (z + dz) % 8)

    above, below = (t, (s + 15) % 16), (t, (s + 1) % 16)
    barrier = pltpu.get_barrier_semaphore()
    near = [at(dz=1), at(dz=7), at(dz=2), at(dz=6), at(dz=4), at(dx=1), at(dx=3)]
    for partner in near + [above, below, at(dc=1)]:
        pl.semaphore_signal(barrier, inc=1, device_id=partner, device_id_type=MESH)

    def greet(step, carry):
        pl.semaphore_signal(
            barrier, inc=1, device_id=((t + 2 * step) % 16, s), device_id_type=MESH
        )
        return carry

    lax.fori_loop(1, 8, greet, 0)

    count = {"sem": 0, "local": 0}
    sent = []

    def take():
        count["sem"] += 1
        return count["sem"] - 1

    def remote(index, src, dst, target):
        return pltpu.make_async_remote_copy(
            src_ref=src, dst_ref=dst, send_sem=send_sem.at[index], recv_sem=recv_sem.at[index],
            device_id=target, device_id_type=MESH,
        )

    def push(index, src, dst, target):
        copy = remote(index, src, dst, target)
        copy.start()
        sent.append(copy)

    def arrive(index, dst):
        remote(index, dst, dst, (t, s)).wait_recv()

    def local(src, dst):
        copy = pltpu.make_async_copy(src, dst, local_sem.at[count["local"]])
        count["local"] += 1
        copy.start()
        return copy

    frames_copy = local(frames, frames_v)
    weights = {
        "q": Weight(wq, wq_v, True),
        "kv": Weight(wkv, wkv_v, False),
        "up0": Weight(wup.at[:, 0:256], wup_v.at[0], True),
        "up1": Weight(wup.at[:, 256:512], wup_v.at[1], True),
        "od": Folded(od_v, ods_v),
    }
    fold_copies = [local(wlat, wlat_v), local(wo, wo_v), local(wdown, wdown_v)]
    own_copy = {kind: local(weights[kind].src, weights[kind].own()) for kind in ("q", "kv") + UPS}
    wconv_copy = local(wconv, wconv_v)

    pl.semaphore_wait(barrier, 17)

    sems = {}

    def far_start(kind):
        w = weights[kind]
        sems[kind, "z"] = take()
        push(sems[kind, "z"], w.src_piece(core, y, x_hi), w.piece(core, y, x), at(dz=4))

    def pair_start(kind):
        w = weights[kind]
        sems[kind, "pair"] = take()
        target = device(core, (x + 3 + 2 * core) % 4, y, z)
        push(sems[kind, "pair"], w.src_half(core), w.pair_half(core), target)

    def pair_share(kind):
        w = weights[kind]
        arrive(sems[kind, "pair"], w.pair_half(core))
        sems[kind, "pair_c"] = take()
        push(sems[kind, "pair_c"], w.pair_half(core), w.pair_half(core), at(dc=1))

    def pair_done(kind):
        arrive(sems[kind, "pair_c"], weights[kind].pair_half(other))

    def row_start(kind):
        w = weights[kind]
        mine = w.piece(core, y, x)
        arrive(sems[kind, "z"], mine)
        for dx in (1, 3, 2):
            sems[kind, "x", dx] = take()
            push(sems[kind, "x", dx], mine, mine, at(dx=dx))

    def column_start(kind):
        w = weights[kind]
        for dx in (1, 3, 2):
            arrive(sems[kind, "x", dx], w.piece(core, y, (x + 4 - dx) % 4))
        mine = w.region(core, y)
        for dy in (1, 3) if kind in UPS else (1, 3, 2):
            sems[kind, "y", dy] = take()
            push(sems[kind, "y", dy], mine, mine, at(dy=dy))
        sems[kind, "c", 0] = take()
        push(sems[kind, "c", 0], mine, mine, at(dc=1))

    def column_relay(kind):
        w = weights[kind]
        for dy, piece in ((1, 0), (3, 1)):
            row = (y + 4 - dy) % 4
            got = w.region(core, row)
            arrive(sems[kind, "y", dy], got)
            half = w.half_region(core, row, piece)
            sems[kind, "y2", dy] = take()
            push(sems[kind, "y2", dy], half, half, at(dy=dy))
            sems[kind, "c", dy] = take()
            push(sems[kind, "c", dy], got, got, at(dc=1))

    def column_share(kind):
        w = weights[kind]
        for dy in (1, 3, 2):
            got = w.region(core, (y + 4 - dy) % 4)
            arrive(sems[kind, "y", dy], got)
            sems[kind, "c", dy] = take()
            push(sems[kind, "c", dy], got, got, at(dc=1))

    def column_end(kind):
        w = weights[kind]
        row = (y + 2) % 4
        for dy, piece in ((1, 0), (3, 1)):
            half = w.half_region(core, row, piece)
            arrive(sems[kind, "y2", dy], half)
            sems[kind, "c2", dy] = take()
            push(sems[kind, "c2", dy], half, half, at(dc=1))

    def far_done(kind):
        w = weights[kind]
        for dy in (0, 1, 3) if kind in UPS else (0, 1, 3, 2):
            arrive(sems[kind, "c", dy], w.region(other, (y + 4 - dy) % 4))
        for dy, piece in ((1, 0), (3, 1)) if kind in UPS else ():
            arrive(sems[kind, "c2", dy], w.half_region(other, (y + 2) % 4, piece))

    for kind in ("q", "kv") + UPS:
        far_start(kind)
    for kind in ("q", "kv"):
        pair_start(kind)

    frames_copy.wait()
    row = lax.broadcasted_iota(jnp.int32, (TOKENS, TOKENS), 0)
    col = lax.broadcasted_iota(jnp.int32, (TOKENS, TOKENS), 1)
    turn = (col == (row & 7) * 16 + (row >> 3)).astype(F32).astype(BF16)
    moved = jnp.dot(turn, frames_v[...], preferred_element_type=F32)
    frame_row = lax.broadcasted_iota(jnp.int32, (8, 2048), 0)
    ids = jnp.zeros((8, 2048), jnp.int32)
    for frame in range(8):
        ids = jnp.where(frame_row == frame, actions[frame], ids)
    embedding = jnp.zeros((8, 2048), F32)
    for action in range(8):
        embedding += jnp.where(ids == action, table[action : action + 1, :].astype(F32), 0.0)
    stream = moved.reshape(16, 8, 2048) + embedding[None]
    x_v[0:128, :] = stream.reshape(TOKENS, 2048).astype(BF16)

    token_sems = {}

    def token_send(name, home, away, dz):
        token_sems[name] = take()
        push(token_sems[name], x_v.at[home], x_v.at[away], at(dz=dz))

    token_send("up first", slice(0, 64), slice(128, 192), 1)
    token_send("down last", slice(64, 128), slice(320, 384), 7)

    def token_arrive(name, away):
        arrive(token_sems[name], x_v.at[away])

    def norm_rows(first, last):
        def block(index, carry):
            rows = pl.ds(pl.multiple_of(index * 16, 16), 16)
            n_v[rows, :] = root_scale(x_v[rows, :].astype(F32), norm_gain[...]).astype(BF16)
            return carry

        lax.fori_loop(first // 16, last // 16, block, 0)

    for copy in fold_copies:
        copy.wait()
    od_v[0:128, :] = jnp.dot(wo_v[...], wlat_v[...], preferred_element_type=F32).astype(BF16)
    od_v[128:640, :] = jnp.dot(wdown_v[...], wlat_v[...], preferred_element_type=F32).astype(BF16)
    token_send("up last", slice(64, 128), slice(192, 256), 1)
    token_send("down first", slice(0, 64), slice(256, 320), 7)
    far_start("od")
    for kind in ("q", "kv"):
        row_start(kind)
    ods_v[0] = od_v[...]
    norm_rows(0, 128)
    token_arrive("up first", slice(128, 192))
    token_send("up on", slice(128, 192), slice(384, 448), 1)
    token_arrive("down last", slice(320, 384))
    token_send("down on", slice(320, 384), slice(448, 512), 7)
    for kind in ("q", "kv"):
        column_start(kind)
    for kind in UPS:
        row_start(kind)
    for kind in ("q", "kv"):
        pair_share(kind)
    for kind in ("q", "kv"):
        column_share(kind)
    for kind in UPS:
        column_start(kind)
    for kind in UPS:
        pair_start(kind)
    token_arrive("up last", slice(192, 256))
    token_arrive("down first", slice(256, 320))
    norm_rows(128, 384)
    row_start("od")
    pair_start("od")
    column_relay("up0")
    token_arrive("up on", slice(384, 448))
    token_arrive("down on", slice(448, 512))
    norm_rows(384, 512)

    column_relay("up1")
    for kind in ("q", "kv"):
        own_copy[kind].wait()
        pair_done(kind)
        far_done(kind)
    routes = (
        (1, slice(0, 128), slice(128, 256)),
        (7, slice(0, 128), slice(256, 384)),
        (2, slice(0, 64), slice(384, 448)),
        (6, slice(64, 128), slice(448, 512)),
    )
    kvt_v[...] = lax.dot_general(
        wkv_v[...], n_v[...], (((1,), (1,)), ((), ())), preferred_element_type=F32
    ).astype(BF16)
    kv_sems = [take() for _ in routes]
    kv_columns = (slice(128, 256), slice(256, 384), slice(384, 512), slice(384, 512))
    for slot, (index, (dz, home, away)) in enumerate(zip(kv_sems, routes)):
        push(index, kvt_v.at[:, kv_columns[slot]], kvr_v.at[slot], at(dz=8 - dz))
    q_sems = [take() for _ in routes]
    q_columns = (slice(512, 1024), slice(1024, 1536), slice(1536, 2048), slice(1536, 2048))
    for half, slots in ((1, (2, 3, 1)), (0, (0,))):
        rows = slice(half * 256, half * 256 + 256)
        q_v[rows, :] = jnp.dot(n_v[rows, :], wq_v[...], preferred_element_type=F32).astype(BF16)
        for slot in slots:
            dz, home, away = routes[slot]
            push(q_sems[slot], q_v.at[away], qr_v.at[home, q_columns[slot]], at(dz=8 - dz))
    qr_v[:, 0:512] = q_v[0:128, :]

    def up_tile(chunk, shard):
        place = chunk * 1024 + shard * 256
        weight = wup_v[chunk, :, shard * 256 : shard * 256 + 256]
        for half in range(2):
            rows = slice(half * 256, half * 256 + 256)
            hidden = jnp.dot(n_v[rows, :], weight, preferred_element_type=F32)
            h_v[rows, place : place + 256] = jax.nn.gelu(hidden, approximate=True).astype(BF16)

    column_start("od")
    for chunk, kind in enumerate(UPS):
        own_copy[kind].wait()
        up_tile(chunk, 0)
    for kind in UPS:
        pair_share(kind)

    for slot, index in enumerate(kv_sems):
        arrive(index, kvr_v.at[slot])
    later_half = lax.broadcasted_iota(jnp.int32, (8, TOKENS), 1) >= 64
    for index, (plane, block) in enumerate((
        (z, kvt_v[:, 0:128].astype(F32)),
        (z + 1, kvr_v[0].astype(F32)),
        (z + 7, kvr_v[1].astype(F32)),
        (z + 2, kvr_v[2].astype(F32)),
        (z + 6, kvr_v[3].astype(F32)),
    )):
        near_plane, far_plane = plane % 8, (plane + 4) % 8
        places = (
            near_plane * 2 + x_lo,
            near_plane * 2 + 1 - x_lo,
            far_plane * 2,
            far_plane * 2 + 1,
        )
        for shard, place in enumerate(places):
            rows = pl.ds(pl.multiple_of(place * 8, 8), 8)
            for part in range(2):
                found = block[shard * 16 + part * 8 : shard * 16 + part * 8 + 8, :]
                if index == 4:
                    found = jnp.where(later_half, found, kvt_f[part, rows, :])
                kvt_f[part, rows, :] = found
    keys = root_scale(jnp.transpose(kvt_f[0]), qk_gain[1:2, :])
    values = jnp.transpose(kvt_f[1])
    kvg_v[t] = jnp.concatenate([keys, values], axis=1).astype(BF16)
    chip = t // 2
    gather_sem, share_sem = count["sem"], count["sem"] + 7
    count["sem"] += 15

    def gather(step):
        mine = kvg_v.at[t]
        return remote(gather_sem + step - 1, mine, mine, ((t + 2 * step) % 16, s))

    def share(step):
        got = kvg_v.at[(t + 16 - 2 * step) % 16]
        return remote(share_sem + step, got, got, at(dc=1))

    def gather_send(step, carry):
        @pl.when(chip + step < 8)
        def _():
            gather(step).start()

        return carry

    def gather_pass(step, carry):
        @pl.when(chip - step >= 0)
        def _():
            arrive(gather_sem + step - 1, kvg_v.at[(t + 16 - 2 * step) % 16])
            share(step).start()

        return carry

    def gather_wait(step, carry):
        @pl.when(chip - step >= 0)
        def _():
            arrive(share_sem + step, kvg_v.at[(t + 16 - 2 * step + 1 - 2 * core) % 16])

        return carry

    def gather_sent(step, carry):
        @pl.when(chip + step < 8)
        def _():
            gather(step).wait_send()

        @pl.when(chip - step >= 0)
        def _():
            share(step).wait_send()

        return carry

    lax.fori_loop(1, 8, gather_send, 0)

    @pl.when(core == 0)
    def _():
        share(0).start()

    for chunk, kind in enumerate(UPS):
        pair_done(kind)
        up_tile(chunk, 1)
    column_share("od")
    column_end("up0")

    for index, (slot, (dz, home, away)) in zip(q_sems, enumerate(routes)):
        arrive(index, qr_v.at[home, q_columns[slot]])
    for head in range(16):
        query = root_scale(qr_v[:, head * 128 : head * 128 + 128].astype(F32), qk_gain[0:1, :])
        qn_v[:, head] = query.astype(BF16).astype(F32).reshape(16, 8, 128)
    lax.fori_loop(1, 8, gather_pass, 0)

    @pl.when(core == 1)
    def _():
        arrive(share_sem, kvg_v.at[t - 1])

    lax.fori_loop(1, 8, gather_wait, 0)

    def widen(index, carry):
        @pl.when(index <= t)
        def _():
            kvf_v[index] = kvg_v[index].astype(F32).reshape(16, 8, 256)

        @pl.when(index > t)
        def _():
            kvf_v[index] = jnp.zeros((16, 8, 256), F32)

        return carry

    lax.fori_loop(0, 16, widen, 0)
    allowed = col <= t * 8 + (row & 7)
    score_scale = 1.0 / math.sqrt(128)

    def attend(place, carry):
        query = qn_v[place].reshape(128, 128).astype(BF16)
        pair = kvf_v[:, place].reshape(128, 256).astype(BF16)
        scores = lax.dot_general(
            query, pair[:, 0:128], (((1,), (1,)), ((), ())), preferred_element_type=F32
        ) * score_scale
        scores = jnp.where(allowed, scores, MASKED)
        exponent = jnp.exp(scores - jnp.max(scores, axis=-1, keepdims=True))
        exponent = jnp.where(allowed, exponent, 0.0)
        totals = jnp.sum(exponent, axis=-1, keepdims=True)
        mixed = jnp.dot(exponent.astype(BF16), pair[:, 128:256], preferred_element_type=F32)
        mixed = mixed / totals
        rows = pl.ds(pl.multiple_of(place * 8, 8), 8)
        for head in range(16):
            ao_f[rows, head * 128 : head * 128 + 128] = mixed[head * 8 : head * 8 + 8, :]
        return carry

    at_sems = []
    sends = (
        ((1, 0, slice(128, 192)), (7, 1, slice(256, 320)), (2, 2, slice(384, 448))),
        ((1, 0, slice(192, 256)), (7, 1, slice(320, 384)), (6, 2, slice(448, 512))),
    )
    for half in range(2):
        lax.fori_loop(half * 8, half * 8 + 8, attend, 0, unroll=4)
        home = slice(half * 64, half * 64 + 64)
        ao_v[home, :] = ao_f[home, :].astype(BF16)
        for dz, slot, away in sends[half]:
            at_sems.append((take(), away))
            push(at_sems[-1][0], ao_v.at[home, q_columns[slot]], at_v.at[away], at(dz=dz))
    at_v[0:128, :] = ao_v[:, 0:512]

    column_end("up1")
    pair_share("od")
    far_done("up0")
    up_tile(0, 2)
    up_tile(0, 3)
    pair_done("od")
    far_done("od")

    def second_layer(rows, blocks):
        total = jnp.zeros((256, 512), F32)
        for place in blocks:
            chunk, shard = place // 4, place % 4
            total += jnp.dot(
                h_v[rows, place * 256 : place * 256 + 256],
                ods_v[shard, 128 + chunk * 256 : 384 + chunk * 256, :],
                preferred_element_type=F32,
            )
        return total

    for half in (1, 0):
        rows = slice(half * 256, half * 256 + 256)
        ffn_f[rows, :] = second_layer(rows, range(6))
    far_done("up1")
    up_tile(1, 2)
    up_tile(1, 3)
    for half in (1, 0):
        rows = slice(half * 256, half * 256 + 256)
        ffn_f[rows, :] += second_layer(rows, (6, 7))
    for index, away in at_sems:
        arrive(index, at_v.at[away])
    sum_sems = [take() for _ in routes]
    places = ((0, slice(0, 128)), (1, slice(0, 128)), (2, slice(0, 64)), (2, slice(64, 128)))
    for half in (1, 0):
        rows = slice(half * 256, half * 256 + 256)
        part = ffn_f[rows, :]
        for shard in range(4):
            part += jnp.dot(
                at_v[rows, shard * 128 : shard * 128 + 128], ods_v[shard, 0:128, :],
                preferred_element_type=F32,
            )
        p_v[rows, :] = part.astype(BF16)
        for slot in ((2, 3, 1), (0,))[1 - half]:
            dz, home, away = routes[slot]
            lead, span = places[slot]
            push(sum_sems[slot], p_v.at[away], pr_v.at[lead, span], at(dz=8 - dz))
    latent = jnp.dot(x_v[0:128, :], wlat_v[...], preferred_element_type=F32)
    latent += p_v[0:128, :].astype(F32)
    for slot, index in enumerate(sum_sems):
        lead, span = places[slot]
        arrive(index, pr_v.at[lead, span])
    for lead in range(3):
        latent += pr_v[lead].astype(F32)
    lat_v[...] = (latent / (1.0 + jnp.exp(-latent))).astype(BF16)
    halo_sem = take()
    push(halo_sem, lat_v, lb_v, above)

    wconv_copy.wait()
    zero_rows = jnp.zeros((8, 512), F32)

    def right_of(cells):
        wide = cells.astype(F32)
        return jnp.concatenate([wide[8:, :], zero_rows], axis=0).astype(BF16)

    def tap(cells, down, across):
        return jnp.dot(cells, wconv_v[down, across], preferred_element_type=F32)

    o_row = lax.broadcasted_iota(jnp.int32, (256, 256), 0)
    o_col = lax.broadcasted_iota(jnp.int32, (256, 256), 1)
    weave = (o_col == (o_row & 1) * 128 + ((o_row >> 1) & 15) * 8 + (o_row >> 5)).astype(F32)
    weave = weave.astype(BF16)

    def store(parity, even, odd):
        pair = jnp.concatenate([even + bias[...], odd + bias[...]], axis=0).astype(BF16)
        woven = jnp.dot(weave, pair, preferred_element_type=F32).astype(BF16)
        out[:, parity] = woven.reshape(8, 32, 512)

    center = lat_v[...]
    right = right_of(center)
    store(0, tap(center, 1, 1), tap(right, 1, 0) + tap(center, 1, 2))
    odd_even = tap(center, 2, 1)
    odd_odd = tap(right, 2, 0) + tap(center, 2, 2)
    arrive(halo_sem, lb_v)
    under = jnp.where(s < 15, lb_v[...].astype(F32), 0.0).astype(BF16)
    corner = right_of(under)
    store(1, odd_even + tap(under, 0, 1), odd_odd + tap(corner, 0, 0) + tap(under, 0, 2))

    for copy in sent:
        copy.wait_send()

    @pl.when(core == 0)
    def _():
        share(0).wait_send()

    lax.fori_loop(1, 8, gather_sent, 0)


def per_device(
    frames, actions, action_table, norm_gain, w_q, w_kv, qk_gain, w_o, w_up, w_down, w_lat, w_conv,
    conv_bias,
):
    w_kv = jnp.transpose(w_kv, (1, 2, 0)).reshape(16, 2048)
    vmem, anywhere = pl.BlockSpec(memory_space=pltpu.VMEM), pl.BlockSpec(memory_space=pl.ANY)
    smem = pl.BlockSpec(memory_space=pltpu.SMEM)
    flops = 2 * 512 * 2048 * (512 * 2 + 64 + 2048 + 512) + 2 * 128 * 512 * (2048 + 9 * 512)
    return pl.pallas_call(
        kernel,
        out_shape=jax.ShapeDtypeStruct((8, 2, 32, 512), BF16),
        in_specs=[
            anywhere, smem, vmem, vmem, anywhere, anywhere, vmem, anywhere, anywhere, anywhere,
            anywhere, anywhere, vmem,
        ],
        out_specs=vmem,
        scratch_shapes=[
            pltpu.VMEM((128, 2048), BF16),
            pltpu.VMEM((2048, 512), BF16),
            pltpu.VMEM((64, 2048), BF16),
            pltpu.VMEM((2, 2048, 1024), BF16),
            pltpu.VMEM((128, 2048), BF16),
            pltpu.VMEM((512, 2048), BF16),
            pltpu.VMEM((2048, 512), BF16),
            pltpu.VMEM((3, 3, 512, 512), BF16),
            pltpu.VMEM((640, 512), BF16),
            pltpu.VMEM((4, 640, 512), BF16),
            pltpu.VMEM((512, 2048), BF16),
            pltpu.VMEM((512, 2048), BF16),
            pltpu.VMEM((512, 512), BF16),
            pltpu.VMEM((128, 2048), BF16),
            pltpu.VMEM((64, 512), BF16),
            pltpu.VMEM((4, 64, 128), BF16),
            pltpu.VMEM((2, 128, 128), F32),
            pltpu.VMEM((16, 128, 256), BF16),
            pltpu.VMEM((16, 16, 8, 256), F32),
            pltpu.VMEM((16, 16, 8, 128), F32),
            pltpu.VMEM((128, 2048), F32),
            pltpu.VMEM((128, 2048), BF16),
            pltpu.VMEM((512, 512), BF16),
            pltpu.VMEM((512, 2048), BF16),
            pltpu.VMEM((512, 512), BF16),
            pltpu.VMEM((3, 128, 512), BF16),
            pltpu.VMEM((512, 512), F32),
            pltpu.VMEM((128, 512), BF16),
            pltpu.VMEM((128, 512), BF16),
            pltpu.SemaphoreType.DMA((N_SEMS,)),
            pltpu.SemaphoreType.DMA((N_SEMS,)),
            pltpu.SemaphoreType.DMA((9,)),
        ],
        compiler_params=pltpu.CompilerParams(
            collective_id=1, has_side_effects=True, vmem_limit_bytes=60 * 1024 * 1024
        ),
        cost_estimate=pl.CostEstimate(flops=flops, bytes_accessed=14000000, transcendentals=0),
        name="block",
    )(
        frames.reshape(128, 2048),
        actions,
        action_table,
        norm_gain.reshape(1, 2048),
        w_q,
        w_kv,
        qk_gain,
        w_o,
        w_up,
        w_down,
        w_lat,
        w_conv,
        conv_bias.reshape(1, 512),
    )


def solution(mesh):
    return jax.shard_map(
        per_device,
        mesh=mesh,
        in_specs=(
            P("tm", "space", None, None),
            P("tm"),
            P(),
            P(),
            P(None, "space"),
            P(None, None, "space"),
            P(),
            P("space", None),
            P(None, "space"),
            P("space", None),
            P(),
            P(),
            P(),
        ),
        out_specs=P("tm", "space", None, None),
        check_vma=False,
    )
```
